128 devices in a mesh: dp: 8 (over z_hi, x), ctx: 16 (over y, z_lo, core).
Axes of the slice: x: 4, y: 4, z: 4 (z_hi: 2, z_lo: 2; z = z_hi * 2 + z_lo), core: 2. Of those that a mesh axis runs over, the one named last changes fastest.
Arguments:
- loaded_x: bfloat16 [16384, 5120], P(('dp', 'ctx')), may hold values from -6 to 6
- dest_dp: int32 [16384], P(('dp', 'ctx')), may hold values from 0 to 7, as said below
- dest_pos: int32 [16384], P(('dp', 'ctx')), may hold values from 0 to 127, as said below
- queries: bfloat16 [16384, 2560], P(('dp', 'ctx')), may hold values from -500 to 500
- grad_out: bfloat16 [16384, 2560], P(('dp', 'ctx')), may hold values from -6 to 6
- kv_weight: bfloat16 [5120, 1024], replicated, may hold values from -0.078125 to 0.078125
- kv_bias: bfloat16 [1024], replicated, may hold values from -3 to 3
- lengths: int32 [8, 4], replicated, may hold values from 1 to 1536, 2048 in all within a row
Outputs:
- attention_out: bfloat16 [16384, 2560], P(('dp', 'ctx'))
- query_grad: bfloat16 [16384, 2560], P(('dp', 'ctx'))
- kv_weight_grad: float32 [5120, 1024], P(('dp', 'ctx'))
The draws below stay inside these ranges and needn't reach their ends.
Inputs may be any that keep to these rules, and one draw needn't show every extreme that they name: `dest_dp`: each loader device sends exactly 16 of its rows to each dp index, always to the device with its own ctx index. `dest_pos`: the rows that reach one device take each of its 128 rows exactly once. `lengths`: each row sums to 2048; its largest entry is 1536.
All inputs are finite; a program needn't handle non-finite values.
Results may differ from the reference program's by a relative error of at most 0.034.
The reference program's roundings to bfloat16 on the way count: a program that leaves them out, or rounds other values in their place, can miss the bound.
Values may be sent and summed in bfloat16 or wider, within the bound.
No kernel may reach another device: no remote copies, remote signals or barrier semaphores. Data moves between devices by JAX's collectives and lax.ppermute only.
A program may use at most 128 MiB of HBM per device.

```python
import math
import jax
import jax.numpy as jnp
import numpy as np
from jax import lax

D = 5120
HD = 128
KV_HEADS = 4
REP = 5
NSEQ = 4
TOK_DEV = 128
KVW = 512
QW = 2560
ROW = 2048
TOKENS = 16384
CAP = 16
MOST = 1536
N_DP = 8
N_CTX = 16


def routing_tables(key):
    device_total = TOKENS // TOK_DEV
    ctx_total = ROW // TOK_DEV
    source_key, target_key = jax.random.split(key)
    source_perm = jax.vmap(lambda sub_key: jax.random.permutation(sub_key, TOK_DEV))(jax.random.split(source_key, device_total))
    target_perm = jax.vmap(lambda sub_key: jax.random.permutation(sub_key, TOK_DEV))(jax.random.split(target_key, device_total))
    device = jnp.arange(device_total, dtype=jnp.int32)[:, None]
    target_dp = (source_perm // CAP).astype(jnp.int32)
    slot_number = (source_perm % CAP).astype(jnp.int32)
    target_device = target_dp * ctx_total + device % ctx_total
    arrival = device // ctx_total * CAP + slot_number
    target_row = target_perm[target_device, arrival].astype(jnp.int32)
    return (target_dp.reshape(TOKENS), target_row.reshape(TOKENS))


def draw_dest_dp(key, part):
    target_dp, target_row = routing_tables(key)
    return target_dp


def draw_dest_pos(key, part):
    target_dp, target_row = routing_tables(key)
    return target_row


def draw_queries(key, part):
    key = jax.random.fold_in(key, 7)
    base_key = jax.random.fold_in(key, 0)
    normal_part = jax.random.normal(base_key, (TOKENS, QW), jnp.float32)
    result = 1.5 * jnp.clip(normal_part, -6.0, 6.0)
    return result.astype(jnp.bfloat16)


def levels(rng, extent, pieces, least, high):
    def one(dim, blocks):
        heights = jax.random.uniform(jax.random.fold_in(jax.random.fold_in(rng, 6), dim), (blocks,), jnp.float32, least / len(pieces), high / len(pieces))
        return jnp.repeat(jnp.exp(heights), extent[dim] // blocks).reshape((-1,) + (1,) * (len(extent) - dim - 1))

    loudness = one(*pieces[0])
    for cut in pieces[1:]:
        loudness = loudness * one(*cut)
    return loudness


def length_profile(amount, total, bound, skew):
    portions = [(1 << 20) // math.isqrt(grade ** skew) + 1 for grade in range(2, amount + 1)]
    spare, given = total - bound - (amount - 1), [1] * (amount - 1)
    while spare > 0:
        movable = [i for i in range(amount - 1) if given[i] < bound]
        pool, remaining = sum([portions[i] for i in movable]), spare
        for i in movable:
            extra = min(bound - given[i], max(1, remaining * portions[i] // pool), spare)
            given[i] = given[i] + extra
            spare = spare - extra
    return np.array([bound] + given)


def ragged_sizes(rng, amount, total, limit, slope):
    if amount == 2:
        one = jax.random.randint(rng, (), max(1, total - limit), min(limit, total - 1) + 1)
        return jnp.stack([one, total - one])
    sizes = jnp.asarray(length_profile(amount, total, limit, slope), jnp.int32)
    twos = (amount - 1) // 2
    giver, taker = sizes[1:1 + 2 * twos:2], sizes[2:2 + 2 * twos:2]
    room = jnp.minimum(giver - 1, limit - taker)
    shifted = jax.random.randint(jax.random.fold_in(rng, 1), (twos,), 0, 1 << 20) % (room + 1)
    sizes = sizes.at[1:1 + 2 * twos:2].set(giver - shifted).at[2:2 + 2 * twos:2].set(taker + shifted)
    return sizes[jax.random.permutation(jax.random.fold_in(rng, 2), amount)]


def noise(rng, extent, scale, limit, shards=(), held_as=jnp.bfloat16):
    drawn = jax.random.normal(rng, extent, jnp.float32) * scale
    if len(shards) > 0:
        drawn = levels(rng, extent, shards, -0.22, 0.18) * drawn
    return jnp.clip(drawn, min=-limit, max=limit).astype(held_as)


def setup_inputs(seed: int = 0) -> dict:
    streams_of = jax.random.split(jax.random.key(seed), 9)
    loaded_x = noise(streams_of[0], (TOKENS, D), 1.0, 6.0, ((0, 128),))
    dest_dp = draw_dest_dp(jax.random.fold_in(streams_of[8], 71), 0)
    dest_pos = draw_dest_pos(jax.random.fold_in(streams_of[8], 71), 0)
    queries = draw_queries(jax.random.fold_in(streams_of[8], 71), 0)
    grad_out = noise(streams_of[4], (TOKENS, QW), 1.0, 6.0, ((0, 128),))
    kv_weight = noise(streams_of[5], (D, 2 * KVW), D ** -0.5, 0.078125)
    kv_bias = noise(streams_of[6], (2 * KVW,), 0.5, 3.0)
    lengths = jax.vmap(lambda own: ragged_sizes(own, NSEQ, ROW, MOST, 2))(jax.random.split(streams_of[7], N_DP)).reshape((N_DP, NSEQ)).astype(jnp.int32)
    return dict(loaded_x=loaded_x, dest_dp=dest_dp, dest_pos=dest_pos, queries=queries, grad_out=grad_out, kv_weight=kv_weight, kv_bias=kv_bias, lengths=lengths)


masked_score = -1e30
rotary_base = 1000000.0


def rotary(flat_rows, position, head_count, direction):
    row_count = flat_rows.shape[0]
    head_width = flat_rows.shape[1] // head_count
    half_width = head_width // 2
    frequency = jnp.power(jnp.float32(rotary_base), -jnp.arange(half_width, dtype=jnp.float32) * (2.0 / head_width))
    angles = position.astype(jnp.float32)[:, None] * frequency[None, :]
    cosine = jnp.cos(angles)[:, None, :]
    sine_part = direction * jnp.sin(angles)[:, None, :]
    shaped = flat_rows.reshape(row_count, head_count, head_width)
    first_half = shaped[..., :half_width]
    second_half = shaped[..., half_width:]
    turned = jnp.concatenate([first_half * cosine - second_half * sine_part, second_half * cosine + first_half * sine_part], axis=-1)
    return turned.reshape(row_count, head_count * head_width)


def query_heads(flat_rows, head_count, repeat):
    row_count = flat_rows.shape[0]
    head_width = flat_rows.shape[1] // (head_count * repeat)
    shaped = flat_rows.reshape(row_count, head_count, repeat, head_width)
    return shaped.transpose(1, 2, 0, 3).reshape(head_count, repeat * row_count, head_width)


def query_rows(stacked, repeat):
    head_count, stacked_rows, head_width = stacked.shape
    row_count = stacked_rows // repeat
    shaped = stacked.reshape(head_count, repeat, row_count, head_width)
    return shaped.transpose(2, 0, 1, 3).reshape(row_count, head_count * repeat * head_width)


def key_heads(flat_rows, head_count):
    row_count = flat_rows.shape[0]
    return flat_rows.reshape(row_count, head_count, flat_rows.shape[1] // head_count).transpose(1, 0, 2)


def key_rows(stacked):
    head_count, row_count, head_width = stacked.shape
    return stacked.transpose(1, 0, 2).reshape(row_count, head_count * head_width)


def reference(loaded_x, dest_dp, dest_pos, queries, grad_out, kv_weight, kv_bias, lengths):
    row_index = jnp.arange(TOKENS, dtype=jnp.int32)
    column = (row_index // TOK_DEV) % N_CTX
    target = ((dest_dp * N_CTX + column) * TOK_DEV + dest_pos).astype(jnp.int32)
    packed = jnp.zeros_like(loaded_x).at[target].set(loaded_x)
    places = jnp.arange(ROW, dtype=jnp.int32)
    seq_ends = jnp.cumsum(lengths, axis=1).astype(jnp.int32)
    starts = jnp.max(jnp.where(seq_ends[:, None, :] <= places[None, :, None], seq_ends[:, None, :], 0), axis=2).astype(jnp.int32)
    position = (places[None, :] - starts).reshape(TOKENS)
    projected = jnp.dot(packed, kv_weight, preferred_element_type=jnp.float32) + kv_bias.astype(jnp.float32)
    rotated_keys = rotary(projected[:, :KVW], position, KV_HEADS, 1.0).astype(jnp.bfloat16)
    value_rows = projected[:, KVW:].astype(jnp.bfloat16)
    score_scale = HD ** -0.5

    def one_group(inputs):
        group_keys, group_values, group_queries, group_grads, group_starts = inputs
        key_stack = key_heads(group_keys, KV_HEADS).astype(jnp.float32)
        value_stack = key_heads(group_values, KV_HEADS).astype(jnp.float32)

        def one_block(running, block):
            block_queries, block_grads, block_places, block_starts = block
            q_stack = query_heads(block_queries, KV_HEADS, REP).astype(jnp.float32)
            g_stack = query_heads(block_grads, KV_HEADS, REP).astype(jnp.float32)
            query_places = jnp.tile(block_places, REP)
            query_starts = jnp.tile(block_starts, REP)
            allowed = (places[None, :] <= query_places[:, None]) & (places[None, :] >= query_starts[:, None])
            scores = jnp.einsum("gqd,gkd->gqk", q_stack, key_stack) * score_scale
            masked = jnp.where(allowed[None], scores, masked_score)
            top_score = jnp.max(masked, axis=-1)
            total_exp = jnp.sum(jnp.where(allowed[None], jnp.exp(masked - top_score[..., None]), 0.0), axis=-1)
            log_total = top_score + jnp.log(total_exp)
            weights = jnp.where(allowed[None], jnp.exp(scores - log_total[..., None]), 0.0)
            rounded = lax.optimization_barrier(weights.astype(jnp.bfloat16)).astype(jnp.float32)
            output_stack = jnp.einsum("gqk,gkd->gqd", rounded, value_stack).astype(jnp.bfloat16)
            delta = jnp.sum(g_stack * output_stack.astype(jnp.float32), axis=-1)
            through = jnp.einsum("gqd,gkd->gqk", g_stack, value_stack)
            slopes = (weights * (through - delta[..., None]) * score_scale).astype(jnp.bfloat16)
            slopes = lax.optimization_barrier(slopes).astype(jnp.float32)
            query_sum = jnp.einsum("gqk,gkd->gqd", slopes, key_stack)
            key_part = jnp.einsum("gqk,gqd->gkd", slopes, q_stack)
            value_part = jnp.einsum("gqk,gqd->gkd", rounded, g_stack)
            block_sums = jnp.concatenate([key_rows(key_part), key_rows(value_part)], axis=1)
            block_sums = lax.optimization_barrier(block_sums.astype(jnp.bfloat16)).astype(jnp.float32)
            attention_block = query_rows(output_stack, REP)
            grad_block = query_rows(query_sum.astype(jnp.bfloat16), REP)
            return running + block_sums, (attention_block, grad_block)

        blocks = (group_queries.reshape(N_CTX, TOK_DEV, QW), group_grads.reshape(N_CTX, TOK_DEV, QW),
                  places.reshape(N_CTX, TOK_DEV), group_starts.reshape(N_CTX, TOK_DEV))
        initial = jnp.zeros((ROW, 2 * KVW), jnp.float32)
        summed, outputs = lax.scan(one_block, initial, blocks)
        return summed, outputs[0].reshape(ROW, QW), outputs[1].reshape(ROW, QW)

    groups = (rotated_keys.reshape(N_DP, ROW, KVW), value_rows.reshape(N_DP, ROW, KVW),
              queries.reshape(N_DP, ROW, QW), grad_out.reshape(N_DP, ROW, QW), starts)
    key_sums, attention_out, query_grad = lax.map(one_group, groups)
    key_sums = key_sums.reshape(TOKENS, 2 * KVW)
    key_part = rotary(key_sums[:, :KVW], position, KV_HEADS, -1.0)
    kv_grad = jnp.concatenate([key_part, key_sums[:, KVW:]], axis=1).astype(jnp.bfloat16)
    kv_weight_grad = jnp.dot(packed.T, kv_grad, preferred_element_type=jnp.float32) * (TOKENS ** -0.5)
    return attention_out.reshape(TOKENS, QW), query_grad.reshape(TOKENS, QW), kv_weight_grad
```

```python
import functools

import jax
import jax.numpy as jnp
import numpy as np
from jax import lax
from jax.experimental import pallas as pl
from jax.experimental.pallas import tpu as pltpu
from jax.sharding import Mesh
from jax.sharding import PartitionSpec as P

D = 5120
HD = 128
HEADS = 4
REP = 5
NSEQ = 4
N_DP = 8
N_Y = 4
N_Q = 4
N_CTX = N_Y * N_Q
ROWS = 128
CAP = ROWS // N_DP
GROUP = N_CTX * ROWS
KVW = HEADS * HD
QH = REP * HD
SHARE = D // (N_DP * N_CTX)
PART = D // N_Q
COLS = 640
CHUNK = 256
N_CHUNK = GROUP // CHUNK
MASKED = -1e30
SCALE = HD**-0.5
LOG2E = 1.4426950408889634
AXES = ("zh", "x", "y", "zl", "c")
DP = ("zh", "x")
Q = ("zl", "c")
bf16 = jnp.bfloat16
f32 = jnp.float32
VMEM_LIMIT = 56 * 1024 * 1024


def iota(shape, axis):
    return lax.broadcasted_iota(jnp.int32, shape, axis)


def dot(a, b):
    return jnp.dot(a, b, preferred_element_type=f32)


def starts_of(places, end_of):
    start = jnp.zeros_like(places)
    for j in range(NSEQ):
        end = end_of(j)
        start = jnp.maximum(start, jnp.where(end <= places, end, 0))
    return start


def project_kernel(where_ref, lengths_ref, dp_ref, pos_ref, freq_ref, bias_ref, x_ref, w_ref,
                   kv_ref, xt_ref, order, total):
    step = pl.program_id(0)

    @pl.when(step == 0)
    def _():
        one_hot = (dp_ref[...] == iota((N_DP, ROWS), 0)).astype(f32)
        before = (iota((ROWS, ROWS), 0) < iota((ROWS, ROWS), 1)).astype(bf16)
        earlier = dot(one_hot.astype(bf16), before)
        rank = jnp.sum(earlier * one_hot, axis=0, keepdims=True).astype(jnp.int32)
        slot = dp_ref[...] * CAP + rank
        order[...] = (iota((ROWS, ROWS), 0) == slot).astype(f32).astype(bf16)
        total[...] = jnp.zeros_like(total)

    rows = dot(order[...], x_ref[...])
    total[...] += dot(rows.astype(bf16), w_ref[...])
    turned = rows.T
    for q in range(N_Q):
        pieces = [
            turned[(j * N_Q + q) * SHARE : (j * N_Q + q + 1) * SHARE] for j in range(COLS // (N_Q * SHARE))
        ]
        xt_ref[q] = jnp.concatenate(pieces, axis=0).astype(bf16)

    @pl.when(step == pl.num_programs(0) - 1)
    def _():
        pos = jnp.sum(order[...].astype(f32) * pos_ref[...].astype(f32), axis=1, keepdims=True)
        pos = jnp.broadcast_to(pos, (ROWS, HD))
        places = pos.astype(jnp.int32) + where_ref[1] * ROWS
        group = iota((ROWS, HD), 0) // CAP
        ends = []
        for b in range(N_DP):
            run = 0
            row = []
            for j in range(NSEQ):
                run = run + lengths_ref[b, j]
                row.append(run)
            ends.append(row)

        def end_of(j):
            end = jnp.zeros((ROWS, HD), jnp.int32)
            for b in range(N_DP):
                end = jnp.where(group == b, ends[b][j], end)
            return end

        angle = (places - starts_of(places, end_of)).astype(f32) * freq_ref[...]
        cosine = jnp.cos(angle)
        sine = jnp.where(iota((ROWS, HD), 1) < HD // 2, -1.0, 1.0) * jnp.sin(angle)
        pos = pos.astype(bf16)
        projected = total[...] + bias_ref[...].astype(f32)
        for g in range(HEADS):
            key = projected[:, g * HD : (g + 1) * HD]
            key = key * cosine + pltpu.roll(key, HD // 2, 1) * sine
            value = projected[:, KVW + g * HD : KVW + (g + 1) * HD]
            packed = jnp.concatenate([key.astype(bf16), value.astype(bf16), pos], axis=1)
            for b in range(N_DP):
                for q in range(N_Q):
                    kv_ref[b, g, q] = packed[b * CAP : (b + 1) * CAP]


def project(where, lengths, dest_dp, dest_pos, freq, bias, x, w):
    smem = pl.BlockSpec(memory_space=pltpu.SMEM)
    whole = lambda *shape: pl.BlockSpec(shape, lambda i: (0,) * len(shape))
    return pl.pallas_call(
        project_kernel,
        grid=(D // COLS,),
        in_specs=[
            smem,
            smem,
            whole(1, ROWS),
            whole(1, ROWS),
            whole(1, HD),
            whole(1, 2 * KVW),
            pl.BlockSpec((ROWS, COLS), lambda i: (0, i)),
            pl.BlockSpec((COLS, 2 * KVW), lambda i: (i, 0)),
        ],
        out_specs=[
            whole(N_DP, HEADS, N_Q, CAP, 3 * HD),
            pl.BlockSpec((N_Q, COLS // N_Q, ROWS), lambda i: (0, i, 0)),
        ],
        out_shape=[
            jax.ShapeDtypeStruct((N_DP, HEADS, N_Q, CAP, 3 * HD), bf16),
            jax.ShapeDtypeStruct((N_Q, PART, ROWS), bf16),
        ],
        scratch_shapes=[pltpu.VMEM((ROWS, ROWS), bf16), pltpu.VMEM((ROWS, 2 * KVW), f32)],
        compiler_params=pltpu.CompilerParams(vmem_limit_bytes=VMEM_LIMIT),
        cost_estimate=pl.CostEstimate(flops=1600000000, bytes_accessed=16000000, transcendentals=0),
        name="project",
    )(where, lengths, dest_dp, dest_pos, freq, bias, x, w)


def attention_kernel(where_ref, lengths_ref, kv_ref, qd_ref, od_ref, dkv_ref, posn_ref,
                     keys, values, keys_t, values_t, places, probs, q_rows, d_rows, q_t, d_t,
                     out_t, dq_t, dk, dv):
    own = where_ref[0]
    q_own = where_ref[2]
    ends = []
    run = 0
    for j in range(NSEQ):
        run = run + lengths_ref[own, j]
        ends.append(run)

    for ctx in range(N_CTX):
        block = kv_ref[:, ctx].reshape(ROWS, 3 * HD)
        rows = slice(ctx * ROWS, (ctx + 1) * ROWS)
        lanes = slice(ctx * ROWS % CHUNK, ctx * ROWS % CHUNK + ROWS)
        key = block[:, :HD]
        value = block[:, HD : 2 * HD]
        keys[rows] = key
        values[rows] = value
        keys_t[ctx * ROWS // CHUNK, :, lanes] = key.astype(f32).T.astype(bf16)
        values_t[ctx * ROWS // CHUNK, :, lanes] = value.astype(f32).T.astype(bf16)
        places[rows] = block[:, 2 * HD :].astype(f32).astype(jnp.int32) + ctx * ROWS
    dk[...] = jnp.zeros_like(dk)
    dv[...] = jnp.zeros_like(dv)

    for y in range(N_Y):
        first = (y * N_Q + q_own) * ROWS
        own_places = places[pl.ds(pl.multiple_of(first, ROWS), ROWS)]
        posn_ref[y] = (own_places - starts_of(own_places, lambda j: ends[j])).astype(f32)
        for h in range(REP):
            lanes = slice(h * HD, (h + 1) * HD)
            query = qd_ref[y, 0, :, lanes]
            cotangent = qd_ref[y, 1, :, lanes]
            q_rows[lanes] = query
            d_rows[lanes] = cotangent
            q_t[:, lanes] = query.astype(f32).T.astype(bf16)
            d_t[:, lanes] = cotangent.astype(f32).T.astype(bf16)
        row_places = first + iota((1, ROWS), 1)
        row_starts = starts_of(row_places, lambda j: ends[j])
        first_start = starts_of(first, lambda j: ends[j])
        low = first_start // CHUNK
        high = (first + ROWS - 1) // CHUNK + 1

        def rows_of(c):
            return pl.ds(pl.multiple_of(c * CHUNK, CHUNK), CHUNK)

        def score(c, top):
            at = rows_of(c)
            key_places = places[at]
            allowed = (key_places <= row_places) & (key_places >= row_starts)
            bias = jnp.where(allowed, 0.0, MASKED)
            s = dot(keys[at], q_t[...]) * (SCALE * LOG2E) + jnp.concatenate([bias] * REP, axis=1)
            probs[at] = s
            return jnp.maximum(top, jnp.max(s, axis=0, keepdims=True))

        top = lax.fori_loop(low, high, score, jnp.full((1, QH), MASKED, f32))
        out_t[...] = jnp.zeros_like(out_t)

        def add_out(c, summed):
            at = rows_of(c)
            p = jnp.exp2(probs[at] - top)
            probs[at] = p
            out_t[...] += dot(values_t[c], p.astype(bf16))
            return summed + jnp.sum(p, axis=0, keepdims=True)

        summed = lax.fori_loop(low, high, add_out, jnp.zeros((1, QH), f32))
        inverse = 1.0 / summed
        rounded = (out_t[...] * inverse).astype(bf16).astype(f32)
        delta = jnp.sum(d_t[...].astype(f32) * rounded, axis=0, keepdims=True)
        for h in range(REP):
            lanes = slice(h * HD, (h + 1) * HD)
            od_ref[y, 0, :, lanes] = rounded[:, lanes].T.astype(bf16)
        dq_t[...] = jnp.zeros_like(dq_t)

        def add_grad(c, carry):
            at = rows_of(c)
            w = probs[at] * inverse
            slope = (w * (dot(values[at], d_t[...]) - delta)).astype(bf16)
            dq_t[...] += dot(keys_t[c], slope)
            dk[at] += dot(slope, q_rows[...])
            dv[at] += dot(w.astype(bf16), d_rows[...])
            return carry

        lax.fori_loop(low, high, add_grad, 0)
        for h in range(REP):
            lanes = slice(h * HD, (h + 1) * HD)
            od_ref[y, 1, :, lanes] = (dq_t[:, lanes] * SCALE).T.astype(bf16)

    for ctx in range(N_CTX):
        rows = slice(ctx * ROWS, (ctx + 1) * ROWS)
        dkv_ref[ctx % N_Q, ctx // N_Q, :, :HD] = (dk[rows] * SCALE).astype(bf16)
        dkv_ref[ctx % N_Q, ctx // N_Q, :, HD:] = dv[rows].astype(bf16)


def attention(where, lengths, kv, qd):
    smem = pl.BlockSpec(memory_space=pltpu.SMEM)
    vmem = pl.BlockSpec(memory_space=pltpu.VMEM)
    return pl.pallas_call(
        attention_kernel,
        in_specs=[smem, smem, vmem, vmem],
        out_specs=[vmem, vmem, vmem],
        out_shape=[
            jax.ShapeDtypeStruct((N_Y, 2, ROWS, QH), bf16),
            jax.ShapeDtypeStruct((N_Q, N_Y, ROWS, 2 * HD), bf16),
            jax.ShapeDtypeStruct((N_Y, ROWS, HD), f32),
        ],
        scratch_shapes=[
            pltpu.VMEM((GROUP, HD), bf16),
            pltpu.VMEM((GROUP, HD), bf16),
            pltpu.VMEM((N_CHUNK, HD, CHUNK), bf16),
            pltpu.VMEM((N_CHUNK, HD, CHUNK), bf16),
            pltpu.VMEM((GROUP, HD), jnp.int32),
            pltpu.VMEM((GROUP, QH), f32),
            pltpu.VMEM((QH, HD), bf16),
            pltpu.VMEM((QH, HD), bf16),
            pltpu.VMEM((HD, QH), bf16),
            pltpu.VMEM((HD, QH), bf16),
            pltpu.VMEM((HD, QH), f32),
            pltpu.VMEM((HD, QH), f32),
            pltpu.VMEM((GROUP, HD), f32),
            pltpu.VMEM((GROUP, HD), f32),
        ],
        compiler_params=pltpu.CompilerParams(vmem_limit_bytes=VMEM_LIMIT),
        cost_estimate=pl.CostEstimate(flops=20000000000, bytes_accessed=8000000, transcendentals=3000000),
        name="attention",
    )(where, lengths, kv, qd)


def key_grad_kernel(parts_ref, cos_ref, sin_ref, out_ref):
    for y in range(N_Y):
        summed = parts_ref[0, y].astype(f32)
        for q in range(1, N_Q):
            summed = summed + parts_ref[q, y].astype(f32)
        key = summed[:, :HD]
        key = key * cos_ref[y] - pltpu.roll(key, HD // 2, 1) * sin_ref[y]
        both = jnp.concatenate([key, summed[:, HD:]], axis=1).astype(bf16)
        for b in range(N_DP):
            for q in range(N_Q):
                out_ref[b, q, y] = both[b * CAP : (b + 1) * CAP]


def key_grad(parts, cosine, sine):
    vmem = pl.BlockSpec(memory_space=pltpu.VMEM)
    return pl.pallas_call(
        key_grad_kernel,
        in_specs=[vmem] * 3,
        out_specs=vmem,
        out_shape=jax.ShapeDtypeStruct((N_DP, N_Q, N_Y, CAP, 2 * HD), bf16),
        compiler_params=pltpu.CompilerParams(vmem_limit_bytes=VMEM_LIMIT),
        name="key_grad",
    )(parts, cosine, sine)


def weight_grad_kernel(xt_ref, kv_ref, out_ref):
    total = None
    for pair in range(N_CTX // 2):
        both = []
        for ctx in (2 * pair, 2 * pair + 1):
            both.append(kv_ref[:, ctx % N_Q, ctx // N_Q].reshape(ROWS, 2 * HD))
        left = jnp.concatenate([xt_ref[2 * pair], xt_ref[2 * pair + 1]], axis=1)
        term = dot(left, jnp.concatenate(both, axis=0))
        total = term if total is None else total + term
    for j in range(out_ref.shape[0]):
        piece = total[j * SHARE : (j + 1) * SHARE]
        out_ref[j] = jnp.concatenate([piece[:, :HD], piece[:, HD:]], axis=0).astype(bf16)


def weight_grad(xt, kv):
    steps = 4
    return pl.pallas_call(
        weight_grad_kernel,
        grid=(steps,),
        in_specs=[
            pl.BlockSpec((N_CTX, PART // steps, ROWS), lambda i: (0, i, 0)),
            pl.BlockSpec((N_DP, N_Q, N_Y, CAP, 2 * HD), lambda i: (0,) * 5),
        ],
        out_specs=pl.BlockSpec((N_DP * N_Y // steps, 2 * SHARE, HD), lambda i: (i, 0, 0)),
        out_shape=jax.ShapeDtypeStruct((N_DP * N_Y, 2 * SHARE, HD), bf16),
        compiler_params=pltpu.CompilerParams(vmem_limit_bytes=VMEM_LIMIT),
        cost_estimate=pl.CostEstimate(flops=1400000000, bytes_accessed=7000000, transcendentals=0),
        name="weight_grad",
    )(xt, kv)


def final_kernel(parts_ref, out_ref):
    for g in range(HEADS):
        summed = parts_ref[0, g].astype(f32)
        for b in range(1, N_DP):
            summed = summed + parts_ref[b, g].astype(f32)
        summed = summed * ((N_DP * GROUP) ** -0.5)
        out_ref[:, g * HD : (g + 1) * HD] = summed[:SHARE]
        out_ref[:, KVW + g * HD : KVW + (g + 1) * HD] = summed[SHARE:]


def final(parts):
    vmem = pl.BlockSpec(memory_space=pltpu.VMEM)
    return pl.pallas_call(
        final_kernel,
        in_specs=[vmem],
        out_specs=vmem,
        out_shape=jax.ShapeDtypeStruct((SHARE, 2 * KVW), f32),
        name="final_sum",
    )(parts)


def swap(array, axes):
    return lax.all_to_all(array, axes, split_axis=0, concat_axis=0, tiled=True)


def shards(loaded_x, dest_dp, dest_pos, queries, grad_out, kv_weight, kv_bias, lengths):
    dp = lax.axis_index(DP)
    y = lax.axis_index("y")
    q = lax.axis_index(Q)
    where = jnp.stack([dp, y * N_Q + q, q]).astype(jnp.int32)
    half = np.power(np.float32(1000000.0), -np.arange(HD // 2, dtype=np.float32) * np.float32(2.0 / HD))
    freq = jnp.asarray(np.concatenate([half, half])[None, :].astype(np.float32))

    qd = jnp.stack([queries, grad_out]).reshape(2, ROWS, HEADS, QH).transpose(2, 0, 1, 3)
    qd = swap(qd, "y")
    kv, xt = project(
        where, lengths, dest_dp.reshape(1, ROWS), dest_pos.reshape(1, ROWS), freq,
        kv_bias.reshape(1, 2 * KVW), loaded_x, kv_weight,
    )
    kv = swap(kv.reshape(N_DP * N_CTX, CAP, 3 * HD), AXES)
    kv, xt = lax.optimization_barrier((kv, xt))
    xt = swap(jnp.broadcast_to(xt[None], (N_Y, N_Q, PART, ROWS)).reshape(N_CTX, PART, ROWS), ("y", "zl", "c"))

    od, dkv, posn = attention(where, lengths, kv.reshape(N_DP, N_CTX, CAP, 3 * HD), qd)
    angle = posn * freq
    cosine = jnp.cos(angle)
    sine = jnp.sin(angle) * jnp.where(jnp.arange(HD) < HD // 2, -1.0, 1.0).astype(f32)
    dkv = swap(dkv, Q)
    od = swap(od, "y")
    kv_grad = key_grad(dkv, cosine, sine)
    kv_grad = swap(kv_grad.reshape(N_DP * N_Q, N_Y * CAP, 2 * HD), ("zh", "x", "zl", "c"))
    dw = weight_grad(xt, kv_grad.reshape(N_DP, N_Q, N_Y, CAP, 2 * HD))
    dw = swap(dw, ("zh", "x", "y"))
    kv_weight_grad = final(dw.reshape(N_DP, HEADS, 2 * SHARE, HD))
    od = od.transpose(1, 2, 0, 3).reshape(2, ROWS, HEADS * QH)
    return od[0], od[1], kv_weight_grad


def solution(mesh):
    split = Mesh(mesh.devices.reshape(2, 4, N_Y, 2, 2), AXES)
    rows = P(AXES, None)
    return jax.shard_map(
        shards,
        mesh=split,
        in_specs=(rows, P(AXES), P(AXES), rows, rows, P(), P(), P()),
        out_specs=(rows, rows, rows),
        check_vma=False,
    )
```

```python
import functools

import jax
import jax.numpy as jnp
import numpy as np
from jax import lax
from jax.experimental import pallas as pl
from jax.experimental.pallas import tpu as pltpu
from jax.sharding import Mesh
from jax.sharding import PartitionSpec as P

D = 5120
HD = 128
HEADS = 4
REP = 5
NSEQ = 4
N_DP = 8
N_Y = 4
N_Q = 4
N_CTX = N_Y * N_Q
ROWS = 128
CAP = ROWS // N_DP
GROUP = N_CTX * ROWS
KVW = HEADS * HD
QH = REP * HD
SHARE = D // (N_DP * N_CTX)
PART = D // N_Q
COLS = 640
TURN = 1280
CHUNK = 256
N_CHUNK = GROUP // CHUNK
MASKED = -1e30
SCALE = HD**-0.5
LOG2E = 1.4426950408889634
AXES = ("zh", "x", "y", "zl", "c")
DP = ("zh", "x")
Q = ("zl", "c")
bf16 = jnp.bfloat16
f32 = jnp.float32
VMEM_LIMIT = 56 * 1024 * 1024


def iota(shape, axis):
    return lax.broadcasted_iota(jnp.int32, shape, axis)


def dot(a, b):
    return jnp.dot(a, b, preferred_element_type=f32)


def starts_of(places, end_of):
    start = jnp.zeros_like(places)
    for j in range(NSEQ):
        end = end_of(j)
        start = jnp.maximum(start, jnp.where(end <= places, end, 0))
    return start


def coordinates():
    dp = lax.axis_index("zh") * 4 + lax.axis_index("x")
    return dp, lax.axis_index("y"), lax.axis_index("zl") * 2 + lax.axis_index("c")


def order_of(dp_row):
    one_hot = (dp_row == iota((N_DP, ROWS), 0)).astype(f32)
    before = (iota((ROWS, ROWS), 0) < iota((ROWS, ROWS), 1)).astype(bf16)
    earlier = dot(one_hot.astype(bf16), before)
    rank = jnp.sum(earlier * one_hot, axis=0, keepdims=True).astype(jnp.int32)
    slot = dp_row * CAP + rank
    return (iota((ROWS, ROWS), 0) == slot).astype(f32).astype(bf16)


def split_kernel(q_ref, d_ref, *out_refs):
    y = lax.axis_index("y")
    for s in range(N_Y):
        lanes = pl.ds(pl.multiple_of(lax.rem(y + s, N_Y) * QH, HD), QH)
        out_refs[s][0] = q_ref[:, lanes]
        out_refs[s][1] = d_ref[:, lanes]


def split_heads(queries, grad_out):
    vmem = pl.BlockSpec(memory_space=pltpu.VMEM)
    return pl.pallas_call(
        split_kernel,
        in_specs=[vmem] * 2,
        out_specs=[vmem] * N_Y,
        out_shape=[jax.ShapeDtypeStruct((2, ROWS, QH), bf16)] * N_Y,
        name="split_heads",
    )(queries, grad_out)


def merge_kernel(*refs):
    y = lax.axis_index("y")
    out_ref, dq_ref = refs[N_Y:]
    for s in range(N_Y):
        lanes = pl.ds(pl.multiple_of(lax.rem(y + s, N_Y) * QH, HD), QH)
        out_ref[:, lanes] = refs[s][0]
        dq_ref[:, lanes] = refs[s][1]


def merge_heads(pieces):
    vmem = pl.BlockSpec(memory_space=pltpu.VMEM)
    return pl.pallas_call(
        merge_kernel,
        in_specs=[vmem] * N_Y,
        out_specs=[vmem] * 2,
        out_shape=[jax.ShapeDtypeStruct((ROWS, HEADS * QH), bf16)] * 2,
        name="merge_heads",
    )(*pieces)


def project_kernel(lengths_ref, dp_ref, pos_ref, freq_ref, bias_ref, x_ref, w_ref, kv_ref, total):
    step = pl.program_id(0)

    @pl.when(step == 0)
    def _():
        total[...] = jnp.zeros_like(total)

    total[...] += dot(x_ref[...], w_ref[...])

    @pl.when(step == pl.num_programs(0) - 1)
    def _():
        _, y, q = coordinates()

        def column(row):
            diagonal = iota((ROWS, ROWS), 0) == iota((ROWS, ROWS), 1)
            picked = jnp.sum(jnp.where(diagonal, row.astype(f32), 0.0), axis=1, keepdims=True)
            return jnp.broadcast_to(picked, (ROWS, HD)).astype(jnp.int32)

        group = column(dp_ref[...])
        pos = column(pos_ref[...])
        places = pos + (y * N_Q + q) * ROWS
        ends = jnp.zeros((N_DP, 1), jnp.int32)
        columns = []
        for j in range(NSEQ):
            ends = ends + lengths_ref[:, j : j + 1]
            columns.append(ends)

        def end_of(j):
            end = jnp.zeros((ROWS, HD), jnp.int32)
            for b in range(N_DP):
                end = jnp.where(group == b, columns[j][b : b + 1], end)
            return end

        angle = (places - starts_of(places, end_of)).astype(f32) * freq_ref[...]
        cosine = jnp.cos(angle)
        sine = jnp.where(iota((ROWS, HD), 1) < HD // 2, -1.0, 1.0) * jnp.sin(angle)
        order = order_of(dp_ref[...])
        bias = bias_ref[...].reshape(1, 2 * KVW).astype(f32)
        pos = pos.astype(f32).astype(bf16)
        for g in range(HEADS):
            lanes = slice(g * HD, (g + 1) * HD)
            key = total[:, lanes] + bias[:, lanes]
            key = key * cosine + pltpu.roll(key, HD // 2, 1) * sine
            lanes = slice(KVW + g * HD, KVW + (g + 1) * HD)
            value = total[:, lanes] + bias[:, lanes]
            packed = jnp.concatenate([key.astype(bf16), value.astype(bf16), pos], axis=1)
            packed = dot(order, packed).astype(bf16)
            for b in range(N_DP):
                for z in range(2):
                    kv_ref[b, g, z] = packed[b * CAP : (b + 1) * CAP]


def project(lengths, dest_dp, dest_pos, freq, bias, x, w):
    whole = lambda *shape: pl.BlockSpec(shape, lambda i: (0,) * len(shape))
    return pl.pallas_call(
        project_kernel,
        grid=(D // COLS,),
        in_specs=[
            whole(N_DP, NSEQ),
            whole(1, ROWS),
            whole(1, ROWS),
            whole(1, HD),
            whole(2 * KVW),
            pl.BlockSpec((ROWS, COLS), lambda i: (0, i)),
            pl.BlockSpec((COLS, 2 * KVW), lambda i: (i, 0)),
        ],
        out_specs=whole(N_DP, HEADS, 2, CAP, 3 * HD),
        out_shape=jax.ShapeDtypeStruct((N_DP, HEADS, 2, CAP, 3 * HD), bf16),
        scratch_shapes=[pltpu.VMEM((ROWS, 2 * KVW), f32)],
        compiler_params=pltpu.CompilerParams(vmem_limit_bytes=VMEM_LIMIT),
        cost_estimate=pl.CostEstimate(flops=1600000000, bytes_accessed=16000000, transcendentals=0),
        name="project",
    )(lengths, dest_dp, dest_pos, freq, bias, x, w)


def turn_kernel(dp_ref, x_ref, *refs):
    out_refs, order, pieces = refs[:N_Q], refs[N_Q], refs[N_Q + 1]
    own = coordinates()[2]

    @pl.when(pl.program_id(0) == 0)
    def _():
        order[...] = order_of(dp_ref[...])

    turned = dot(order[...], x_ref[...]).T
    for q in range(N_Q):
        rows = [turned[(j * N_Q + q) * SHARE : (j * N_Q + q + 1) * SHARE] for j in range(TURN // (N_Q * SHARE))]
        pieces[q] = jnp.concatenate(rows, axis=0).astype(bf16)
    for m in range(N_Q):
        out_refs[m][...] = pieces[own ^ m]


def turn(dest_dp, x):
    return pl.pallas_call(
        turn_kernel,
        grid=(D // TURN,),
        in_specs=[
            pl.BlockSpec((1, ROWS), lambda i: (0, 0)),
            pl.BlockSpec((ROWS, TURN), lambda i: (0, i)),
        ],
        out_specs=[pl.BlockSpec((TURN // N_Q, ROWS), lambda i: (i, 0))] * N_Q,
        out_shape=[jax.ShapeDtypeStruct((PART, ROWS), bf16)] * N_Q,
        scratch_shapes=[pltpu.VMEM((ROWS, ROWS), bf16), pltpu.VMEM((N_Q, TURN // N_Q, ROWS), bf16)],
        compiler_params=pltpu.CompilerParams(vmem_limit_bytes=VMEM_LIMIT),
        cost_estimate=pl.CostEstimate(flops=2000000000, bytes_accessed=2600000, transcendentals=0),
        name="turn",
    )(dest_dp, x)


def attention_kernel(lengths_ref, kv_own_ref, kv_other_ref, *refs):
    qd_refs, od_refs, dkv_refs = refs[:N_Y], refs[N_Y : 2 * N_Y], refs[2 * N_Y : 2 * N_Y + N_Q]
    posn_ref = refs[2 * N_Y + N_Q]
    (keys, values, keys_t, values_t, places, probs, q_rows, d_rows, q_t, d_t,
                     out_t, dq_t, dk, dv) = refs[2 * N_Y + N_Q + 1 :]
    own, y_own, q_own = coordinates()
    ends = []
    for j in range(NSEQ):
        counted = (iota((N_DP, NSEQ), 0) == own) & (iota((N_DP, NSEQ), 1) <= j)
        ends.append(jnp.sum(jnp.where(counted, lengths_ref[...], 0).astype(f32)).astype(jnp.int32))

    core = q_own % 2
    for kv_ref, c in ((kv_own_ref, core), (kv_other_ref, 1 - core)):
        for chunk in range(N_CHUNK):
            block = kv_ref[:, chunk // 2, chunk % 2].reshape(ROWS, 3 * HD)
            first = pl.multiple_of(chunk * CHUNK + c * ROWS, ROWS)
            rows = pl.ds(first, ROWS)
            lanes = pl.ds(pl.multiple_of(c * ROWS, ROWS), ROWS)
            key = block[:, :HD]
            value = block[:, HD : 2 * HD]
            keys[rows] = key
            values[rows] = value
            keys_t[chunk, :, lanes] = key.astype(f32).T.astype(bf16)
            values_t[chunk, :, lanes] = value.astype(f32).T.astype(bf16)
            places[rows] = block[:, 2 * HD :].astype(f32).astype(jnp.int32) + first
    dk[...] = jnp.zeros_like(dk)
    dv[...] = jnp.zeros_like(dv)

    for s in range(N_Y):
        qd_ref, od_ref = qd_refs[s], od_refs[s]
        own_places = places[pl.ds(pl.multiple_of((s * N_Q + q_own) * ROWS, ROWS), ROWS)]
        first = (lax.rem(y_own + N_Y - s, N_Y) * N_Q + q_own) * ROWS
        posn_ref[s] = (own_places - starts_of(own_places, lambda j: ends[j])).astype(f32)
        for h in range(REP):
            lanes = slice(h * HD, (h + 1) * HD)
            query = qd_ref[0, :, lanes]
            cotangent = qd_ref[1, :, lanes]
            q_rows[lanes] = query
            d_rows[lanes] = cotangent
            q_t[:, lanes] = query.astype(f32).T.astype(bf16)
            d_t[:, lanes] = cotangent.astype(f32).T.astype(bf16)
        row_places = first + iota((1, ROWS), 1)
        row_starts = starts_of(row_places, lambda j: ends[j])
        first_start = starts_of(first, lambda j: ends[j])
        low = first_start // CHUNK
        high = (first + ROWS - 1) // CHUNK + 1

        def rows_of(c):
            return pl.ds(pl.multiple_of(c * CHUNK, CHUNK), CHUNK)

        def score(c, top):
            at = rows_of(c)
            key_places = places[at]
            allowed = (key_places <= row_places) & (key_places >= row_starts)
            bias = jnp.where(allowed, 0.0, MASKED)
            s = dot(keys[at], q_t[...]) * (SCALE * LOG2E) + jnp.concatenate([bias] * REP, axis=1)
            probs[at] = s
            return jnp.maximum(top, jnp.max(s, axis=0, keepdims=True))

        top = lax.fori_loop(low, high, score, jnp.full((1, QH), MASKED, f32))
        out_t[...] = jnp.zeros_like(out_t)

        def add_out(c, summed):
            at = rows_of(c)
            p = jnp.exp2(probs[at] - top)
            probs[at] = p
            out_t[...] += dot(values_t[c], p.astype(bf16))
            return summed + jnp.sum(p, axis=0, keepdims=True)

        summed = lax.fori_loop(low, high, add_out, jnp.zeros((1, QH), f32))
        inverse = 1.0 / summed
        rounded = (out_t[...] * inverse).astype(bf16).astype(f32)
        delta = jnp.sum(d_t[...].astype(f32) * rounded, axis=0, keepdims=True)
        for h in range(REP):
            lanes = slice(h * HD, (h + 1) * HD)
            od_ref[0, :, lanes] = rounded[:, lanes].T.astype(bf16)
        dq_t[...] = jnp.zeros_like(dq_t)

        def add_grad(c, carry):
            at = rows_of(c)
            w = probs[at] * inverse
            slope = (w * (dot(values[at], d_t[...]) - delta)).astype(bf16)
            dq_t[...] += dot(keys_t[c], slope)
            dk[at] += dot(slope, q_rows[...])
            dv[at] += dot(w.astype(bf16), d_rows[...])
            return carry

        lax.fori_loop(low, high, add_grad, 0)
        for h in range(REP):
            lanes = slice(h * HD, (h + 1) * HD)
            od_ref[1, :, lanes] = (dq_t[:, lanes] * SCALE).T.astype(bf16)

    for m in range(N_Q):
        for y in range(N_Y):
            rows = pl.ds(pl.multiple_of((y * N_Q + (q_own ^ m)) * ROWS, ROWS), ROWS)
            dkv_refs[m][y, :, :HD] = (dk[rows] * SCALE).astype(bf16)
            dkv_refs[m][y, :, HD:] = dv[rows].astype(bf16)


def attention(lengths, kv_own, kv_other, qd):
    vmem = pl.BlockSpec(memory_space=pltpu.VMEM)
    return pl.pallas_call(
        attention_kernel,
        in_specs=[vmem] * (3 + N_Y),
        out_specs=[vmem] * (N_Y + N_Q + 1),
        out_shape=[jax.ShapeDtypeStruct((2, ROWS, QH), bf16)] * N_Y
        + [jax.ShapeDtypeStruct((N_Y, ROWS, 2 * HD), bf16)] * N_Q
        + [jax.ShapeDtypeStruct((N_Y, ROWS, HD), f32)],
        scratch_shapes=[
            pltpu.VMEM((GROUP, HD), bf16),
            pltpu.VMEM((GROUP, HD), bf16),
            pltpu.VMEM((N_CHUNK, HD, CHUNK), bf16),
            pltpu.VMEM((N_CHUNK, HD, CHUNK), bf16),
            pltpu.VMEM((GROUP, HD), jnp.int32),
            pltpu.VMEM((GROUP, QH), f32),
            pltpu.VMEM((QH, HD), bf16),
            pltpu.VMEM((QH, HD), bf16),
            pltpu.VMEM((HD, QH), bf16),
            pltpu.VMEM((HD, QH), bf16),
            pltpu.VMEM((HD, QH), f32),
            pltpu.VMEM((HD, QH), f32),
            pltpu.VMEM((GROUP, HD), f32),
            pltpu.VMEM((GROUP, HD), f32),
        ],
        compiler_params=pltpu.CompilerParams(vmem_limit_bytes=VMEM_LIMIT),
        cost_estimate=pl.CostEstimate(flops=20000000000, bytes_accessed=8000000, transcendentals=3000000),
        name="attention",
    )(lengths, kv_own, kv_other, *qd)


def key_grad_kernel(cos_ref, sin_ref, *refs):
    out_ref = refs[N_Q]
    for y in range(N_Y):
        summed = refs[0][y].astype(f32)
        for q in range(1, N_Q):
            summed = summed + refs[q][y].astype(f32)
        key = summed[:, :HD]
        key = key * cos_ref[y] - pltpu.roll(key, HD // 2, 1) * sin_ref[y]
        both = jnp.concatenate([key, summed[:, HD:]], axis=1).astype(bf16)
        for b in range(N_DP):
            for z in range(2):
                out_ref[b, z, y] = both[b * CAP : (b + 1) * CAP]


def key_grad(parts, cosine, sine):
    vmem = pl.BlockSpec(memory_space=pltpu.VMEM)
    return pl.pallas_call(
        key_grad_kernel,
        in_specs=[vmem] * (2 + N_Q),
        out_specs=vmem,
        out_shape=jax.ShapeDtypeStruct((N_DP, 2, N_Y, CAP, 2 * HD), bf16),
        compiler_params=pltpu.CompilerParams(vmem_limit_bytes=VMEM_LIMIT),
        name="key_grad",
    )(cosine, sine, *parts)


def weight_grad_kernel(kv_own_ref, kv_other_ref, xt_ref, out_ref):
    zl = lax.axis_index("zl")
    total = None
    for y in range(N_Y):
        for z in range(2):
            kv = [ref[:, zl ^ z, y].reshape(ROWS, 2 * HD) for ref in (kv_own_ref, kv_other_ref)]
            left = jnp.concatenate([xt_ref[y, 2 * z], xt_ref[y, 2 * z + 1]], axis=1)
            term = dot(left, jnp.concatenate(kv, axis=0))
            total = term if total is None else total + term
    for j in range(out_ref.shape[0]):
        piece = total[j * SHARE : (j + 1) * SHARE]
        out_ref[j] = jnp.concatenate([piece[:, :HD], piece[:, HD:]], axis=0).astype(bf16)


def weight_grad(xt, kv_own, kv_other):
    steps = 4
    return pl.pallas_call(
        weight_grad_kernel,
        grid=(steps,),
        in_specs=[
            pl.BlockSpec((N_DP, 2, N_Y, CAP, 2 * HD), lambda i: (0,) * 5),
            pl.BlockSpec((N_DP, 2, N_Y, CAP, 2 * HD), lambda i: (0,) * 5),
            pl.BlockSpec((N_Y, N_Q, PART // steps, ROWS), lambda i: (0, 0, i, 0)),
        ],
        out_specs=pl.BlockSpec((N_DP * N_Y // steps, 2 * SHARE, HD), lambda i: (i, 0, 0)),
        out_shape=jax.ShapeDtypeStruct((N_DP * N_Y, 2 * SHARE, HD), bf16),
        compiler_params=pltpu.CompilerParams(vmem_limit_bytes=VMEM_LIMIT),
        cost_estimate=pl.CostEstimate(flops=1400000000, bytes_accessed=7000000, transcendentals=0),
        name="weight_grad",
    )(kv_own, kv_other, xt)


def final_kernel(parts_ref, out_ref):
    for g in range(HEADS):
        summed = parts_ref[0, g].astype(f32)
        for b in range(1, N_DP):
            summed = summed + parts_ref[b, g].astype(f32)
        summed = summed * ((N_DP * GROUP) ** -0.5)
        out_ref[:, g * HD : (g + 1) * HD] = summed[:SHARE]
        out_ref[:, KVW + g * HD : KVW + (g + 1) * HD] = summed[SHARE:]


def final(parts):
    vmem = pl.BlockSpec(memory_space=pltpu.VMEM)
    return pl.pallas_call(
        final_kernel,
        in_specs=[vmem],
        out_specs=vmem,
        out_shape=jax.ShapeDtypeStruct((SHARE, 2 * KVW), f32),
        name="final_sum",
    )(parts)


def swap(array, axes):
    return lax.all_to_all(array, axes, split_axis=0, concat_axis=0, tiled=True)


def flip(array, m):
    return lax.ppermute(array, Q, [(i, i ^ m) for i in range(N_Q)])


def along_y(array, s):
    return lax.ppermute(array, "y", [(i, (i + s) % N_Y) for i in range(N_Y)])


def shards(loaded_x, dest_dp, dest_pos, queries, grad_out, kv_weight, kv_bias, lengths):
    half = np.power(np.float32(1000000.0), -np.arange(HD // 2, dtype=np.float32) * np.float32(2.0 / HD))
    freq = jnp.asarray(np.concatenate([half, half])[None, :].astype(np.float32))
    dest_dp = dest_dp.reshape(1, ROWS)

    xt = turn(dest_dp, loaded_x)
    queries, xt = lax.optimization_barrier((queries, xt))
    qd = split_heads(queries, grad_out)
    x, qd, xt = lax.optimization_barrier((loaded_x, qd, xt))
    xt = [xt[0]] + [flip(xt[m], m) for m in range(1, N_Q)]
    qd = [qd[0]] + [along_y(qd[s], s) for s in range(1, N_Y)]
    kv = project(lengths, dest_dp, dest_pos.reshape(1, ROWS), freq, kv_bias, x, kv_weight)
    kv, xt, qd = lax.optimization_barrier((kv, xt, qd))
    xt = jnp.stack(xt)
    kv, xt = lax.optimization_barrier((kv, xt))
    xt = lax.all_gather(xt, "y", axis=0)
    kv = swap(kv.reshape(-1, CAP, 3 * HD), ("zh", "x", "y", "zl")).reshape(N_DP, N_Y, 2, CAP, 3 * HD)
    kv_other = lax.ppermute(kv, "c", [(0, 1), (1, 0)])

    results = attention(lengths, kv, kv_other, qd)
    od, dkv, posn = results[:N_Y], results[N_Y : N_Y + N_Q], results[-1]
    angle = posn * freq
    cosine = jnp.cos(angle)
    sine = jnp.sin(angle) * jnp.where(jnp.arange(HD) < HD // 2, -1.0, 1.0).astype(f32)
    dkv = [dkv[0]] + [flip(dkv[m], m) for m in range(1, N_Q)]
    od = [od[0]] + [along_y(od[s], -s) for s in range(1, N_Y)]
    dkv, od = lax.optimization_barrier((dkv, od))
    kv_grad = key_grad(dkv, cosine, sine)
    kv_grad = swap(kv_grad.reshape(-1, N_Y * CAP, 2 * HD), ("zh", "x", "zl")).reshape(N_DP, 2, N_Y, CAP, 2 * HD)
    attention_out, query_grad = merge_heads(od)
    kv_grad, attention_out, query_grad = lax.optimization_barrier((kv_grad, attention_out, query_grad))
    kv_grad_other = lax.ppermute(kv_grad, "c", [(0, 1), (1, 0)])
    dw = weight_grad(xt, kv_grad, kv_grad_other)
    dw = swap(dw, ("zh", "x", "y"))
    kv_weight_grad = final(dw.reshape(N_DP, HEADS, 2 * SHARE, HD))
    return attention_out, query_grad, kv_weight_grad


def solution(mesh):
    split = Mesh(mesh.devices.reshape(2, 4, N_Y, 2, 2), AXES)
    rows = P(AXES, None)
    return jax.shard_map(
        shards,
        mesh=split,
        in_specs=(rows, P(AXES), P(AXES), rows, rows, P(), P(), P()),
        out_specs=(rows, rows, rows),
        check_vma=False,
    )
```

```python
import functools

import jax
import jax.numpy as jnp
import numpy as np
from jax import lax
from jax.experimental import pallas as pl
from jax.experimental.pallas import tpu as pltpu
from jax.sharding import Mesh
from jax.sharding import PartitionSpec as P

D = 5120
HD = 128
HEADS = 4
REP = 5
NSEQ = 4
N_DP = 8
N_Y = 4
N_Q = 4
N_CTX = N_Y * N_Q
ROWS = 128
CAP = ROWS // N_DP
GROUP = N_CTX * ROWS
KVW = HEADS * HD
QH = REP * HD
SHARE = D // (N_DP * N_CTX)
PART = D // N_Q
COLS = 2560
TURN = 2560
CHUNK = 512
PAIR = 2 * ROWS
N_CHUNK = GROUP // CHUNK
MASKED = -1e30
SCALE = HD**-0.5
LOG2E = 1.4426950408889634
AXES = ("zh", "x", "y", "zl", "c")
DP = ("zh", "x")
Q = ("zl", "c")
bf16 = jnp.bfloat16
f32 = jnp.float32
VMEM_LIMIT = 56 * 1024 * 1024


def iota(shape, axis):
    return lax.broadcasted_iota(jnp.int32, shape, axis)


def dot(a, b):
    return jnp.dot(a, b, preferred_element_type=f32)


def starts_of(places, end_of):
    start = jnp.zeros_like(places)
    for j in range(NSEQ):
        end = end_of(j)
        start = jnp.maximum(start, jnp.where(end <= places, end, 0))
    return start


def coordinates():
    dp = lax.axis_index("zh") * 4 + lax.axis_index("x")
    return dp, lax.axis_index("y"), lax.axis_index("zl") * 2 + lax.axis_index("c")


def order_of(dp_row):
    one_hot = (dp_row == iota((N_DP, ROWS), 0)).astype(f32)
    before = (iota((ROWS, ROWS), 0) < iota((ROWS, ROWS), 1)).astype(bf16)
    earlier = dot(one_hot.astype(bf16), before)
    rank = jnp.sum(earlier * one_hot, axis=0, keepdims=True).astype(jnp.int32)
    slot = dp_row * CAP + rank
    return (iota((ROWS, ROWS), 0) == slot).astype(f32).astype(bf16)


def cut_kernel(dp_ref, x_ref, q_ref, d_ref, *refs):
    head_refs, piece_refs, order, pieces = refs[:N_Y], refs[N_Y : N_Y + N_Q], refs[-2], refs[-1]
    _, y, own = coordinates()

    @pl.when(pl.program_id(0) == 0)
    def _():
        order[...] = order_of(dp_ref[...])

    for s in range(N_Y):
        lanes = pl.ds(pl.multiple_of(lax.rem(y + s, N_Y) * QH, HD), QH)
        head_refs[s][0] = q_ref[:, lanes]
        head_refs[s][1] = d_ref[:, lanes]
    turned = dot(order[...], x_ref[...]).T
    for q in range(N_Q):
        rows = [turned[(j * N_Q + q) * SHARE : (j * N_Q + q + 1) * SHARE] for j in range(TURN // (N_Q * SHARE))]
        pieces[q] = jnp.concatenate(rows, axis=0).astype(bf16)
    for m in range(N_Q):
        piece_refs[m][...] = pieces[own ^ m]


def cut(dest_dp, x, queries, grad_out):
    steps = D // TURN
    rows = ROWS // steps
    return pl.pallas_call(
        cut_kernel,
        grid=(steps,),
        in_specs=[
            pl.BlockSpec((1, ROWS), lambda i: (0, 0)),
            pl.BlockSpec((ROWS, TURN), lambda i: (0, i)),
            pl.BlockSpec((rows, HEADS * QH), lambda i: (i, 0)),
            pl.BlockSpec((rows, HEADS * QH), lambda i: (i, 0)),
        ],
        out_specs=[pl.BlockSpec((2, rows, QH), lambda i: (0, i, 0))] * N_Y
        + [pl.BlockSpec((TURN // N_Q, ROWS), lambda i: (i, 0))] * N_Q,
        out_shape=[jax.ShapeDtypeStruct((2, ROWS, QH), bf16)] * N_Y
        + [jax.ShapeDtypeStruct((PART, ROWS), bf16)] * N_Q,
        scratch_shapes=[pltpu.VMEM((ROWS, ROWS), bf16), pltpu.VMEM((N_Q, TURN // N_Q, ROWS), bf16)],
        compiler_params=pltpu.CompilerParams(vmem_limit_bytes=VMEM_LIMIT),
        cost_estimate=pl.CostEstimate(flops=2000000000, bytes_accessed=5200000, transcendentals=0),
        name="cut",
    )(dest_dp, x, queries, grad_out)


def merge_kernel(stay_ref, back_ref, ahead_ref, dq_ref, out_ref, *refs):
    y = lax.axis_index("y")
    pieces = [
        (stay_ref.at[0], stay_ref.at[1]),
        (back_ref.at[0], back_ref.at[1]),
        (out_ref.at[0], dq_ref.at[0]),
        (ahead_ref.at[0], ahead_ref.at[1]),
    ]
    for s in range(N_Y):
        lanes = pl.ds(pl.multiple_of(lax.rem(y + s, N_Y) * QH, HD), QH)
        for k in range(2):
            refs[k][:, lanes] = pieces[s][k][...]


def merge_heads(*pieces):
    vmem = pl.BlockSpec(memory_space=pltpu.VMEM)
    return pl.pallas_call(
        merge_kernel,
        in_specs=[vmem] * len(pieces),
        out_specs=[vmem] * 2,
        out_shape=[jax.ShapeDtypeStruct((ROWS, HEADS * QH), bf16)] * 2,
        name="merge_heads",
    )(*pieces)


def project_kernel(lengths_ref, dp_ref, pos_ref, freq_ref, bias_ref, x_ref, w_ref, kv_ref, total):
    step = pl.program_id(0)

    @pl.when(step == 0)
    def _():
        total[...] = jnp.zeros_like(total)

    total[...] += dot(x_ref[...], w_ref[...])

    @pl.when(step == pl.num_programs(0) - 1)
    def _():
        _, y, q = coordinates()

        def column(row):
            diagonal = iota((ROWS, ROWS), 0) == iota((ROWS, ROWS), 1)
            picked = jnp.sum(jnp.where(diagonal, row.astype(f32), 0.0), axis=1, keepdims=True)
            return jnp.broadcast_to(picked, (ROWS, HD)).astype(jnp.int32)

        group = column(dp_ref[...])
        pos = column(pos_ref[...])
        places = pos + (y * N_Q + q) * ROWS
        ends = jnp.zeros((N_DP, 1), jnp.int32)
        columns = []
        for j in range(NSEQ):
            ends = ends + lengths_ref[:, j : j + 1]
            columns.append(ends)

        def end_of(j):
            end = jnp.zeros((ROWS, HD), jnp.int32)
            for b in range(N_DP):
                end = jnp.where(group == b, columns[j][b : b + 1], end)
            return end

        angle = (places - starts_of(places, end_of)).astype(f32) * freq_ref[...]
        cosine = jnp.cos(angle)
        sine = jnp.where(iota((ROWS, HD), 1) < HD // 2, -1.0, 1.0) * jnp.sin(angle)
        order = order_of(dp_ref[...])
        bias = bias_ref[...].reshape(1, 2 * KVW).astype(f32)
        pos = pos.astype(f32).astype(bf16)
        for g in range(HEADS):
            lanes = slice(g * HD, (g + 1) * HD)
            key = total[:, lanes] + bias[:, lanes]
            key = key * cosine + pltpu.roll(key, HD // 2, 1) * sine
            lanes = slice(KVW + g * HD, KVW + (g + 1) * HD)
            value = total[:, lanes] + bias[:, lanes]
            packed = jnp.concatenate([key.astype(bf16), value.astype(bf16), pos], axis=1)
            packed = dot(order, packed).astype(bf16)
            for b in range(N_DP):
                for z in range(2):
                    kv_ref[b, g, z] = packed[b * CAP : (b + 1) * CAP]


def project(lengths, dest_dp, dest_pos, freq, bias, x, w):
    whole = lambda *shape: pl.BlockSpec(shape, lambda i: (0,) * len(shape))
    return pl.pallas_call(
        project_kernel,
        grid=(D // COLS,),
        in_specs=[
            whole(N_DP, NSEQ),
            whole(1, ROWS),
            whole(1, ROWS),
            whole(1, HD),
            whole(2 * KVW),
            pl.BlockSpec((ROWS, COLS), lambda i: (0, i)),
            pl.BlockSpec((COLS, 2 * KVW), lambda i: (i, 0)),
        ],
        out_specs=whole(N_DP, HEADS, 2, CAP, 3 * HD),
        out_shape=jax.ShapeDtypeStruct((N_DP, HEADS, 2, CAP, 3 * HD), bf16),
        scratch_shapes=[pltpu.VMEM((ROWS, 2 * KVW), f32)],
        compiler_params=pltpu.CompilerParams(vmem_limit_bytes=VMEM_LIMIT),
        cost_estimate=pl.CostEstimate(flops=1600000000, bytes_accessed=16000000, transcendentals=0),
        name="project",
    )(lengths, dest_dp, dest_pos, freq, bias, x, w)


def attention_kernel(lengths_ref, kv_own_ref, kv_other_ref, *refs):
    qd_refs, refs = refs[:N_Y], refs[N_Y:]
    stay_ref, back_ref, ahead_ref = refs[:3]
    out_refs = [stay_ref.at[0], back_ref.at[0], ahead_ref.at[2], ahead_ref.at[0]]
    dq_refs = [stay_ref.at[1], back_ref.at[1], back_ref.at[2], ahead_ref.at[1]]
    dkv_refs = refs[3 : 3 + N_Q]
    posn_ref = refs[3 + N_Q]
    (keys, values, keys_t, values_t, places, probs, q_rows, d_rows, q_t, d_t,
                     out_t, dq_t, dk, dv) = refs[4 + N_Q :]
    own, y_own, q_own = coordinates()
    ends = []
    for j in range(NSEQ):
        counted = (iota((N_DP, NSEQ), 0) == own) & (iota((N_DP, NSEQ), 1) <= j)
        ends.append(jnp.sum(jnp.where(counted, lengths_ref[...], 0).astype(f32)).astype(jnp.int32))

    core = q_own % 2
    for kv_ref, c in ((kv_own_ref, core), (kv_other_ref, 1 - core)):
        for pair in range(GROUP // PAIR):
            block = kv_ref[:, pair // 2, pair % 2].reshape(ROWS, 3 * HD)
            first = pl.multiple_of(pair * PAIR + c * ROWS, ROWS)
            rows = pl.ds(first, ROWS)
            chunk = pair * PAIR // CHUNK
            lanes = pl.ds(pl.multiple_of(pair * PAIR % CHUNK + c * ROWS, ROWS), ROWS)
            key = block[:, :HD]
            value = block[:, HD : 2 * HD]
            keys[rows] = key
            values[rows] = value
            keys_t[chunk, :, lanes] = key.T
            values_t[chunk, :, lanes] = value.T
            places[rows] = block[:, 2 * HD :].astype(f32).astype(jnp.int32) + first
    dk[...] = jnp.zeros_like(dk)
    dv[...] = jnp.zeros_like(dv)

    for s in range(N_Y):
        qd_ref = qd_refs[s]
        own_places = places[pl.ds(pl.multiple_of((s * N_Q + q_own) * ROWS, ROWS), ROWS)]
        first = (lax.rem(y_own + N_Y - s, N_Y) * N_Q + q_own) * ROWS
        posn_ref[s] = (own_places - starts_of(own_places, lambda j: ends[j])).astype(f32)
        for h in range(REP):
            lanes = slice(h * HD, (h + 1) * HD)
            query = qd_ref[0, :, lanes]
            cotangent = qd_ref[1, :, lanes]
            q_rows[lanes] = query
            d_rows[lanes] = cotangent
            q_t[:, lanes] = query.T
            d_t[:, lanes] = cotangent.T
        row_places = first + iota((1, ROWS), 1)
        row_starts = starts_of(row_places, lambda j: ends[j])
        first_start = starts_of(first, lambda j: ends[j])
        low = first_start // CHUNK
        high = (first + ROWS - 1) // CHUNK + 1

        def rows_of(c):
            return pl.ds(pl.multiple_of(c * CHUNK, CHUNK), CHUNK)

        def score(c, top):
            at = rows_of(c)
            key_places = places[at]
            allowed = (key_places <= row_places) & (key_places >= row_starts)
            bias = jnp.where(allowed, 0.0, MASKED)
            s = dot(keys[at], q_t[...]) * (SCALE * LOG2E) + jnp.concatenate([bias] * REP, axis=1)
            probs[at] = s
            return jnp.maximum(top, jnp.max(s, axis=0, keepdims=True))

        top = lax.fori_loop(low, high, score, jnp.full((1, QH), MASKED, f32))
        out_t[...] = jnp.zeros_like(out_t)

        def add_out(c, summed):
            at = rows_of(c)
            p = jnp.exp2(probs[at] - top)
            probs[at] = p
            out_t[...] += dot(values_t[c], p.astype(bf16))
            return summed + jnp.sum(p, axis=0, keepdims=True)

        summed = lax.fori_loop(low, high, add_out, jnp.zeros((1, QH), f32))
        inverse = 1.0 / summed
        rounded = (out_t[...] * inverse).astype(bf16).astype(f32)
        delta = jnp.sum(d_t[...].astype(f32) * rounded, axis=0, keepdims=True)
        for h in range(REP):
            lanes = slice(h * HD, (h + 1) * HD)
            out_refs[s][:, lanes] = rounded[:, lanes].astype(bf16).T
        dq_t[...] = jnp.zeros_like(dq_t)

        def add_grad(c, carry):
            at = rows_of(c)
            w = probs[at] * inverse
            slope = (w * (dot(values[at], d_t[...]) - delta)).astype(bf16)
            dq_t[...] += dot(keys_t[c], slope)
            dk[at] += dot(slope, q_rows[...])
            dv[at] += dot(w.astype(bf16), d_rows[...])
            return carry

        lax.fori_loop(low, high, add_grad, 0)
        for h in range(REP):
            lanes = slice(h * HD, (h + 1) * HD)
            dq_refs[s][:, lanes] = (dq_t[:, lanes] * SCALE).astype(bf16).T

    for m in range(N_Q):
        for y in range(N_Y):
            rows = pl.ds(pl.multiple_of((y * N_Q + (q_own ^ m)) * ROWS, ROWS), ROWS)
            dkv_refs[m][y, :, :HD] = (dk[rows] * SCALE).astype(bf16)
            dkv_refs[m][y, :, HD:] = dv[rows].astype(bf16)


def attention(lengths, kv_own, kv_other, qd):
    vmem = pl.BlockSpec(memory_space=pltpu.VMEM)
    return pl.pallas_call(
        attention_kernel,
        in_specs=[vmem] * (3 + N_Y),
        out_specs=[vmem] * (4 + N_Q),
        out_shape=[jax.ShapeDtypeStruct((n, ROWS, QH), bf16) for n in (2, 3, 3)]
        + [jax.ShapeDtypeStruct((N_Y, ROWS, 2 * HD), bf16)] * N_Q
        + [jax.ShapeDtypeStruct((N_Y, ROWS, HD), f32)],
        scratch_shapes=[
            pltpu.VMEM((GROUP, HD), bf16),
            pltpu.VMEM((GROUP, HD), bf16),
            pltpu.VMEM((N_CHUNK, HD, CHUNK), bf16),
            pltpu.VMEM((N_CHUNK, HD, CHUNK), bf16),
            pltpu.VMEM((GROUP, HD), jnp.int32),
            pltpu.VMEM((GROUP, QH), f32),
            pltpu.VMEM((QH, HD), bf16),
            pltpu.VMEM((QH, HD), bf16),
            pltpu.VMEM((HD, QH), bf16),
            pltpu.VMEM((HD, QH), bf16),
            pltpu.VMEM((HD, QH), f32),
            pltpu.VMEM((HD, QH), f32),
            pltpu.VMEM((GROUP, HD), f32),
            pltpu.VMEM((GROUP, HD), f32),
        ],
        compiler_params=pltpu.CompilerParams(vmem_limit_bytes=VMEM_LIMIT),
        cost_estimate=pl.CostEstimate(flops=20000000000, bytes_accessed=8000000, transcendentals=3000000),
        name="attention",
    )(lengths, kv_own, kv_other, *qd)


def key_grad_kernel(cos_ref, sin_ref, *refs):
    out_ref = refs[N_Q]
    for y in range(N_Y):
        summed = refs[0][y].astype(f32)
        for q in range(1, N_Q):
            summed = summed + refs[q][y].astype(f32)
        key = summed[:, :HD]
        key = key * cos_ref[y] - pltpu.roll(key, HD // 2, 1) * sin_ref[y]
        both = jnp.concatenate([key, summed[:, HD:]], axis=1).astype(bf16)
        for b in range(N_DP):
            for z in range(2):
                out_ref[b, z, y] = both[b * CAP : (b + 1) * CAP]


def key_grad(parts, cosine, sine):
    vmem = pl.BlockSpec(memory_space=pltpu.VMEM)
    return pl.pallas_call(
        key_grad_kernel,
        in_specs=[vmem] * (2 + N_Q),
        out_specs=vmem,
        out_shape=jax.ShapeDtypeStruct((N_DP, 2, N_Y, CAP, 2 * HD), bf16),
        compiler_params=pltpu.CompilerParams(vmem_limit_bytes=VMEM_LIMIT),
        name="key_grad",
    )(cosine, sine, *parts)


def weight_grad_kernel(kv_own_ref, kv_other_ref, xt_ref, out_ref):
    zl = lax.axis_index("zl")
    total = None
    for y in range(N_Y):
        for z in range(2):
            kv = [ref[:, zl ^ z, y].reshape(ROWS, 2 * HD) for ref in (kv_own_ref, kv_other_ref)]
            left = jnp.concatenate([xt_ref[y, 2 * z], xt_ref[y, 2 * z + 1]], axis=1)
            term = dot(left, jnp.concatenate(kv, axis=0))
            total = term if total is None else total + term
    for j in range(out_ref.shape[0]):
        piece = total[j * SHARE : (j + 1) * SHARE]
        out_ref[j] = jnp.concatenate([piece[:, :HD], piece[:, HD:]], axis=0).astype(bf16)


def weight_grad(xt, kv_own, kv_other):
    steps = 2
    return pl.pallas_call(
        weight_grad_kernel,
        grid=(steps,),
        in_specs=[
            pl.BlockSpec((N_DP, 2, N_Y, CAP, 2 * HD), lambda i: (0,) * 5),
            pl.BlockSpec((N_DP, 2, N_Y, CAP, 2 * HD), lambda i: (0,) * 5),
            pl.BlockSpec((N_Y, N_Q, PART // steps, ROWS), lambda i: (0, 0, i, 0)),
        ],
        out_specs=pl.BlockSpec((N_DP * N_Y // steps, 2 * SHARE, HD), lambda i: (i, 0, 0)),
        out_shape=jax.ShapeDtypeStruct((N_DP * N_Y, 2 * SHARE, HD), bf16),
        compiler_params=pltpu.CompilerParams(vmem_limit_bytes=VMEM_LIMIT),
        cost_estimate=pl.CostEstimate(flops=1400000000, bytes_accessed=7000000, transcendentals=0),
        name="weight_grad",
    )(kv_own, kv_other, xt)


def final_kernel(parts_ref, out_ref):
    for g in range(HEADS):
        summed = parts_ref[0, g].astype(f32)
        for b in range(1, N_DP):
            summed = summed + parts_ref[b, g].astype(f32)
        summed = summed * ((N_DP * GROUP) ** -0.5)
        out_ref[:, g * HD : (g + 1) * HD] = summed[:SHARE]
        out_ref[:, KVW + g * HD : KVW + (g + 1) * HD] = summed[SHARE:]


def final(parts):
    vmem = pl.BlockSpec(memory_space=pltpu.VMEM)
    return pl.pallas_call(
        final_kernel,
        in_specs=[vmem],
        out_specs=vmem,
        out_shape=jax.ShapeDtypeStruct((SHARE, 2 * KVW), f32),
        name="final_sum",
    )(parts)


def swap(array, axes):
    return lax.all_to_all(array, axes, split_axis=0, concat_axis=0, tiled=True)


def flip(array, m):
    return lax.ppermute(array, Q, [(i, i ^ m) for i in range(N_Q)])


def along_y(array, s):
    return lax.ppermute(array, "y", [(i, (i + s) % N_Y) for i in range(N_Y)])


def shards(loaded_x, dest_dp, dest_pos, queries, grad_out, kv_weight, kv_bias, lengths):
    half = np.power(np.float32(1000000.0), -np.arange(HD // 2, dtype=np.float32) * np.float32(2.0 / HD))
    freq = jnp.asarray(np.concatenate([half, half])[None, :].astype(np.float32))
    dest_dp = dest_dp.reshape(1, ROWS)

    barrier = lax.optimization_barrier

    pieces = cut(dest_dp, loaded_x, queries, grad_out)
    x, qd, xt = barrier((loaded_x, pieces[:N_Y], pieces[N_Y:]))
    xt = [xt[0]] + [flip(xt[m], m) for m in range(1, N_Q)]
    qd = [qd[0]] + [along_y(qd[s], s) for s in range(1, N_Y)]
    kv = project(lengths, dest_dp, dest_pos.reshape(1, ROWS), freq, kv_bias, x, kv_weight)
    kv, xt = barrier((kv, xt))
    xt = jnp.stack(xt)
    kv, xt, qd = barrier((kv, xt, qd))
    xt = lax.all_gather(xt, "y", axis=0)
    kv = swap(kv.reshape(-1, CAP, 3 * HD), ("zh", "x", "y", "zl")).reshape(N_DP, N_Y, 2, CAP, 3 * HD)
    kv_other = lax.ppermute(kv, "c", [(0, 1), (1, 0)])

    stay, back, ahead, *dkv, posn = attention(lengths, kv, kv_other, qd)
    angle = posn * freq
    cosine = jnp.cos(angle)
    sine = jnp.sin(angle) * jnp.where(jnp.arange(HD) < HD // 2, -1.0, 1.0).astype(f32)
    dkv = [dkv[0]] + [flip(dkv[m], m) for m in range(1, N_Q)]
    back, ahead = along_y(back, -1), along_y(ahead, 1)
    kv_grad = key_grad(dkv, cosine, sine)
    kv_grad, back, ahead = barrier((kv_grad, back, ahead))
    kv_grad = swap(kv_grad.reshape(-1, N_Y * CAP, 2 * HD), ("zh", "x", "zl")).reshape(N_DP, 2, N_Y, CAP, 2 * HD)
    kv_grad_other = lax.ppermute(kv_grad, "c", [(0, 1), (1, 0)])
    last_dq, last_out = along_y(back[2:], -1), along_y(ahead[2:], 1)
    dw = weight_grad(xt, kv_grad, kv_grad_other)
    dw, last_dq, last_out = barrier((dw, last_dq, last_out))
    dw = swap(dw, ("zh", "x", "y"))
    attention_out, query_grad = merge_heads(stay, back, ahead, last_dq, last_out)
    dw, attention_out, query_grad = barrier((dw, attention_out, query_grad))
    kv_weight_grad = final(dw.reshape(N_DP, HEADS, 2 * SHARE, HD))
    return attention_out, query_grad, kv_weight_grad


def solution(mesh):
    split = Mesh(mesh.devices.reshape(2, 4, N_Y, 2, 2), AXES)
    rows = P(AXES, None)
    return jax.shard_map(
        shards,
        mesh=split,
        in_specs=(rows, P(AXES), P(AXES), rows, rows, P(), P(), P()),
        out_specs=(rows, rows, rows),
        check_vma=False,
    )
```

```python
import functools

import jax
import jax.numpy as jnp
import numpy as np
from jax import lax
from jax.experimental import pallas as pl
from jax.experimental.pallas import tpu as pltpu
from jax.sharding import Mesh
from jax.sharding import PartitionSpec as P

D = 5120
HD = 128
HEADS = 4
REP = 5
NSEQ = 4
N_DP = 8
N_Y = 4
N_Q = 4
N_CTX = N_Y * N_Q
ROWS = 128
CAP = ROWS // N_DP
GROUP = N_CTX * ROWS
KVW = HEADS * HD
QH = REP * HD
SHARE = D // (N_DP * N_CTX)
PART = D // N_Q
COLS = 2560
TURN = 2560
CHUNK = 512
PAIR = 2 * ROWS
N_CHUNK = GROUP // CHUNK
MASKED = -1e30
SCALE = HD**-0.5
LOG2E = 1.4426950408889634
AXES = ("zh", "x", "y", "zl", "c")
DP = ("zh", "x")
Q = ("zl", "c")
bf16 = jnp.bfloat16
f32 = jnp.float32
VMEM_LIMIT = 56 * 1024 * 1024


def iota(shape, axis):
    return lax.broadcasted_iota(jnp.int32, shape, axis)


def dot(a, b):
    return jnp.dot(a, b, preferred_element_type=f32)


def starts_of(places, end_of):
    start = jnp.zeros_like(places)
    for j in range(NSEQ):
        end = end_of(j)
        start = jnp.maximum(start, jnp.where(end <= places, end, 0))
    return start


def coordinates():
    dp = lax.axis_index("zh") * 4 + lax.axis_index("x")
    return dp, lax.axis_index("y"), lax.axis_index("zl") * 2 + lax.axis_index("c")


def order_of(dp_row):
    one_hot = (dp_row == iota((N_DP, ROWS), 0)).astype(f32)
    before = (iota((ROWS, ROWS), 0) < iota((ROWS, ROWS), 1)).astype(bf16)
    earlier = dot(one_hot.astype(bf16), before)
    rank = jnp.sum(earlier * one_hot, axis=0, keepdims=True).astype(jnp.int32)
    slot = dp_row * CAP + rank
    return (iota((ROWS, ROWS), 0) == slot).astype(f32).astype(bf16)


def cut_kernel(dp_ref, x_ref, q_ref, d_ref, *refs):
    head_refs, piece_refs, order, pieces = refs[:N_Y], refs[N_Y : N_Y + N_Q], refs[-2], refs[-1]
    _, y, own = coordinates()

    @pl.when(pl.program_id(0) == 0)
    def _():
        order[...] = order_of(dp_ref[...])

    for s in range(N_Y):
        lanes = pl.ds(pl.multiple_of(lax.rem(y + s, N_Y) * QH, HD), QH)
        head_refs[s][0] = q_ref[:, lanes]
        head_refs[s][1] = d_ref[:, lanes]
    turned = dot(order[...], x_ref[...]).T
    for q in range(N_Q):
        rows = [turned[(j * N_Q + q) * SHARE : (j * N_Q + q + 1) * SHARE] for j in range(TURN // (N_Q * SHARE))]
        pieces[q] = jnp.concatenate(rows, axis=0).astype(bf16)
    for m in range(N_Q):
        piece_refs[m][...] = pieces[own ^ m]


def cut(dest_dp, x, queries, grad_out):
    steps = D // TURN
    rows = ROWS // steps
    return pl.pallas_call(
        cut_kernel,
        grid=(steps,),
        in_specs=[
            pl.BlockSpec((1, ROWS), lambda i: (0, 0)),
            pl.BlockSpec((ROWS, TURN), lambda i: (0, i)),
            pl.BlockSpec((rows, HEADS * QH), lambda i: (i, 0)),
            pl.BlockSpec((rows, HEADS * QH), lambda i: (i, 0)),
        ],
        out_specs=[pl.BlockSpec((2, rows, QH), lambda i: (0, i, 0))] * N_Y
        + [pl.BlockSpec((TURN // N_Q, ROWS), lambda i: (i, 0))] * N_Q,
        out_shape=[jax.ShapeDtypeStruct((2, ROWS, QH), bf16)] * N_Y
        + [jax.ShapeDtypeStruct((PART, ROWS), bf16)] * N_Q,
        scratch_shapes=[pltpu.VMEM((ROWS, ROWS), bf16), pltpu.VMEM((N_Q, TURN // N_Q, ROWS), bf16)],
        compiler_params=pltpu.CompilerParams(vmem_limit_bytes=VMEM_LIMIT),
        cost_estimate=pl.CostEstimate(flops=2000000000, bytes_accessed=5200000, transcendentals=0),
        name="cut",
    )(dest_dp, x, queries, grad_out)


def merge_kernel(stay_ref, back_ref, ahead_ref, dq_ref, out_ref, *refs):
    y = lax.axis_index("y")
    pieces = [
        (stay_ref.at[0], stay_ref.at[1]),
        (back_ref.at[0], back_ref.at[1]),
        (out_ref.at[0], dq_ref.at[0]),
        (ahead_ref.at[0], ahead_ref.at[1]),
    ]
    for s in range(N_Y):
        lanes = pl.ds(pl.multiple_of(lax.rem(y + s, N_Y) * QH, HD), QH)
        for k in range(2):
            refs[k][:, lanes] = pieces[s][k][...]


def merge_heads(*pieces):
    vmem = pl.BlockSpec(memory_space=pltpu.VMEM)
    return pl.pallas_call(
        merge_kernel,
        in_specs=[vmem] * len(pieces),
        out_specs=[vmem] * 2,
        out_shape=[jax.ShapeDtypeStruct((ROWS, HEADS * QH), bf16)] * 2,
        name="merge_heads",
    )(*pieces)


def project_kernel(lengths_ref, dp_ref, pos_ref, freq_ref, bias_ref, x_ref, w_ref, kv_ref, total):
    step = pl.program_id(0)

    @pl.when(step == 0)
    def _():
        total[...] = jnp.zeros_like(total)

    total[...] += dot(x_ref[...], w_ref[...])

    @pl.when(step == pl.num_programs(0) - 1)
    def _():
        _, y, q = coordinates()

        def column(row):
            diagonal = iota((ROWS, ROWS), 0) == iota((ROWS, ROWS), 1)
            picked = jnp.sum(jnp.where(diagonal, row.astype(f32), 0.0), axis=1, keepdims=True)
            return jnp.broadcast_to(picked, (ROWS, HD)).astype(jnp.int32)

        group = column(dp_ref[...])
        pos = column(pos_ref[...])
        places = pos + (y * N_Q + q) * ROWS
        ends = jnp.zeros((N_DP, 1), jnp.int32)
        columns = []
        for j in range(NSEQ):
            ends = ends + lengths_ref[:, j : j + 1]
            columns.append(ends)

        def end_of(j):
            end = jnp.zeros((ROWS, HD), jnp.int32)
            for b in range(N_DP):
                end = jnp.where(group == b, columns[j][b : b + 1], end)
            return end

        angle = (places - starts_of(places, end_of)).astype(f32) * freq_ref[...]
        cosine = jnp.cos(angle)
        sine = jnp.where(iota((ROWS, HD), 1) < HD // 2, -1.0, 1.0) * jnp.sin(angle)
        order = order_of(dp_ref[...])
        bias = bias_ref[...].reshape(1, 2 * KVW).astype(f32)
        pos = pos.astype(f32).astype(bf16)
        for g in range(HEADS):
            lanes = slice(g * HD, (g + 1) * HD)
            key = total[:, lanes] + bias[:, lanes]
            key = key * cosine + pltpu.roll(key, HD // 2, 1) * sine
            lanes = slice(KVW + g * HD, KVW + (g + 1) * HD)
            value = total[:, lanes] + bias[:, lanes]
            packed = jnp.concatenate([key.astype(bf16), value.astype(bf16), pos], axis=1)
            packed = dot(order, packed).astype(bf16)
            for b in range(N_DP):
                for z in range(2):
                    kv_ref[b, g, z] = packed[b * CAP : (b + 1) * CAP]


def project(lengths, dest_dp, dest_pos, freq, bias, x, w):
    whole = lambda *shape: pl.BlockSpec(shape, lambda i: (0,) * len(shape))
    return pl.pallas_call(
        project_kernel,
        grid=(D // COLS,),
        in_specs=[
            whole(N_DP, NSEQ),
            whole(1, ROWS),
            whole(1, ROWS),
            whole(1, HD),
            whole(2 * KVW),
            pl.BlockSpec((ROWS, COLS), lambda i: (0, i)),
            pl.BlockSpec((COLS, 2 * KVW), lambda i: (i, 0)),
        ],
        out_specs=whole(N_DP, HEADS, 2, CAP, 3 * HD),
        out_shape=jax.ShapeDtypeStruct((N_DP, HEADS, 2, CAP, 3 * HD), bf16),
        scratch_shapes=[pltpu.VMEM((ROWS, 2 * KVW), f32)],
        compiler_params=pltpu.CompilerParams(vmem_limit_bytes=VMEM_LIMIT),
        cost_estimate=pl.CostEstimate(flops=1600000000, bytes_accessed=16000000, transcendentals=0),
        name="project",
    )(lengths, dest_dp, dest_pos, freq, bias, x, w)


def attention_kernel(lengths_ref, kv_own_ref, kv_other_ref, *refs):
    qd_refs, refs = refs[:N_Y], refs[N_Y:]
    stay_ref, back_ref, ahead_ref = refs[:3]
    out_refs = [stay_ref.at[0], back_ref.at[0], ahead_ref.at[2], ahead_ref.at[0]]
    dq_refs = [stay_ref.at[1], back_ref.at[1], back_ref.at[2], ahead_ref.at[1]]
    dkv_refs = refs[3 : 3 + N_Q]
    posn_ref = refs[3 + N_Q]
    (keys, values, keys_t, values_t, places, probs, q_rows, d_rows, q_t, d_t,
                     out_t, dq_t, dk, dv) = refs[4 + N_Q :]
    own, y_own, q_own = coordinates()
    ends = []
    for j in range(NSEQ):
        counted = (iota((N_DP, NSEQ), 0) == own) & (iota((N_DP, NSEQ), 1) <= j)
        ends.append(jnp.sum(jnp.where(counted, lengths_ref[...], 0).astype(f32)).astype(jnp.int32))

    core = q_own % 2
    for kv_ref, c in ((kv_own_ref, core), (kv_other_ref, 1 - core)):
        for pair in range(GROUP // PAIR):
            block = kv_ref[:, pair // 2, pair % 2].reshape(ROWS, 3 * HD)
            first = pl.multiple_of(pair * PAIR + c * ROWS, ROWS)
            rows = pl.ds(first, ROWS)
            chunk = pair * PAIR // CHUNK
            lanes = pl.ds(pl.multiple_of(pair * PAIR % CHUNK + c * ROWS, ROWS), ROWS)
            key = block[:, :HD]
            value = block[:, HD : 2 * HD]
            keys[rows] = key
            values[rows] = value
            keys_t[chunk, :, lanes] = key.T
            values_t[chunk, :, lanes] = value.T
            places[rows] = block[:, 2 * HD :].astype(f32).astype(jnp.int32) + first
    dk[...] = jnp.zeros_like(dk)
    dv[...] = jnp.zeros_like(dv)

    for s in range(N_Y):
        qd_ref = qd_refs[s]
        own_places = places[pl.ds(pl.multiple_of((s * N_Q + q_own) * ROWS, ROWS), ROWS)]
        first = (lax.rem(y_own + N_Y - s, N_Y) * N_Q + q_own) * ROWS
        posn_ref[s] = (own_places - starts_of(own_places, lambda j: ends[j])).astype(f32)
        for h in range(REP):
            lanes = slice(h * HD, (h + 1) * HD)
            query = qd_ref[0, :, lanes]
            cotangent = qd_ref[1, :, lanes]
            q_rows[lanes] = query
            d_rows[lanes] = cotangent
            q_t[:, lanes] = query.T
            d_t[:, lanes] = cotangent.T
        row_places = first + iota((1, ROWS), 1)
        row_starts = starts_of(row_places, lambda j: ends[j])
        first_start = starts_of(first, lambda j: ends[j])
        low = first_start // CHUNK
        high = (first + ROWS - 1) // CHUNK + 1

        def rows_of(c):
            return pl.ds(pl.multiple_of(c * CHUNK, CHUNK), CHUNK)

        def score(c, top):
            at = rows_of(c)
            key_places = places[at]
            allowed = (key_places <= row_places) & (key_places >= row_starts)
            bias = jnp.where(allowed, 0.0, MASKED)
            s = dot(keys[at], q_t[...]) * (SCALE * LOG2E) + jnp.concatenate([bias] * REP, axis=1)
            probs[at] = s
            return jnp.maximum(top, jnp.max(s, axis=0, keepdims=True))

        top = lax.fori_loop(low, high, score, jnp.full((1, QH), MASKED, f32))
        out_t[...] = jnp.zeros_like(out_t)

        def add_out(c, summed):
            at = rows_of(c)
            p = jnp.exp2(probs[at] - top)
            probs[at] = p
            out_t[...] += dot(values_t[c], p.astype(bf16))
            return summed + jnp.sum(p, axis=0, keepdims=True)

        summed = lax.fori_loop(low, high, add_out, jnp.zeros((1, QH), f32))
        inverse = 1.0 / summed
        rounded = (out_t[...] * inverse).astype(bf16).astype(f32)
        delta = jnp.sum(d_t[...].astype(f32) * rounded, axis=0, keepdims=True)
        for h in range(REP):
            lanes = slice(h * HD, (h + 1) * HD)
            out_refs[s][:, lanes] = rounded[:, lanes].astype(bf16).T
        dq_t[...] = jnp.zeros_like(dq_t)

        def add_grad(c, carry):
            at = rows_of(c)
            w = probs[at] * inverse
            slope = (w * (dot(values[at], d_t[...]) - delta)).astype(bf16)
            dq_t[...] += dot(keys_t[c], slope)
            dk[at] += dot(slope, q_rows[...])
            dv[at] += dot(w.astype(bf16), d_rows[...])
            return carry

        lax.fori_loop(low, high, add_grad, 0)
        for h in range(REP):
            lanes = slice(h * HD, (h + 1) * HD)
            dq_refs[s][:, lanes] = (dq_t[:, lanes] * SCALE).astype(bf16).T

    for m in range(N_Q):
        for y in range(N_Y):
            rows = pl.ds(pl.multiple_of((y * N_Q + (q_own ^ m)) * ROWS, ROWS), ROWS)
            dkv_refs[m][y, :, :HD] = (dk[rows] * SCALE).astype(bf16)
            dkv_refs[m][y, :, HD:] = dv[rows].astype(bf16)


def attention(lengths, kv_own, kv_other, qd):
    vmem = pl.BlockSpec(memory_space=pltpu.VMEM)
    return pl.pallas_call(
        attention_kernel,
        in_specs=[vmem] * (3 + N_Y),
        out_specs=[vmem] * (4 + N_Q),
        out_shape=[jax.ShapeDtypeStruct((n, ROWS, QH), bf16) for n in (2, 3, 3)]
        + [jax.ShapeDtypeStruct((N_Y, ROWS, 2 * HD), bf16)] * N_Q
        + [jax.ShapeDtypeStruct((N_Y, ROWS, HD), f32)],
        scratch_shapes=[
            pltpu.VMEM((GROUP, HD), bf16),
            pltpu.VMEM((GROUP, HD), bf16),
            pltpu.VMEM((N_CHUNK, HD, CHUNK), bf16),
            pltpu.VMEM((N_CHUNK, HD, CHUNK), bf16),
            pltpu.VMEM((GROUP, HD), jnp.int32),
            pltpu.VMEM((GROUP, QH), f32),
            pltpu.VMEM((QH, HD), bf16),
            pltpu.VMEM((QH, HD), bf16),
            pltpu.VMEM((HD, QH), bf16),
            pltpu.VMEM((HD, QH), bf16),
            pltpu.VMEM((HD, QH), f32),
            pltpu.VMEM((HD, QH), f32),
            pltpu.VMEM((GROUP, HD), f32),
            pltpu.VMEM((GROUP, HD), f32),
        ],
        compiler_params=pltpu.CompilerParams(vmem_limit_bytes=VMEM_LIMIT),
        cost_estimate=pl.CostEstimate(flops=20000000000, bytes_accessed=8000000, transcendentals=3000000),
        name="attention",
    )(lengths, kv_own, kv_other, *qd)


def key_grad_kernel(cos_ref, sin_ref, *refs):
    out_ref = refs[N_Q]
    for y in range(N_Y):
        summed = refs[0][y].astype(f32)
        for q in range(1, N_Q):
            summed = summed + refs[q][y].astype(f32)
        key = summed[:, :HD]
        key = key * cos_ref[y] - pltpu.roll(key, HD // 2, 1) * sin_ref[y]
        both = jnp.concatenate([key, summed[:, HD:]], axis=1).astype(bf16)
        for b in range(N_DP):
            for z in range(2):
                out_ref[b, z, y] = both[b * CAP : (b + 1) * CAP]


def key_grad(parts, cosine, sine):
    vmem = pl.BlockSpec(memory_space=pltpu.VMEM)
    return pl.pallas_call(
        key_grad_kernel,
        in_specs=[vmem] * (2 + N_Q),
        out_specs=vmem,
        out_shape=jax.ShapeDtypeStruct((N_DP, 2, N_Y, CAP, 2 * HD), bf16),
        compiler_params=pltpu.CompilerParams(vmem_limit_bytes=VMEM_LIMIT),
        name="key_grad",
    )(cosine, sine, *parts)


def weight_grad_kernel(kv_own_ref, kv_other_ref, xt_ref, out_ref):
    zl = lax.axis_index("zl")
    total = None
    for y in range(N_Y):
        for z in range(2):
            kv = [ref[:, zl ^ z, y].reshape(ROWS, 2 * HD) for ref in (kv_own_ref, kv_other_ref)]
            left = jnp.concatenate([xt_ref[y, 2 * z], xt_ref[y, 2 * z + 1]], axis=1)
            term = dot(left, jnp.concatenate(kv, axis=0))
            total = term if total is None else total + term
    for j in range(out_ref.shape[0]):
        piece = total[j * SHARE : (j + 1) * SHARE]
        out_ref[j] = jnp.concatenate([piece[:, :HD], piece[:, HD:]], axis=0).astype(bf16)


def weight_grad(xt, kv_own, kv_other):
    steps = 2
    return pl.pallas_call(
        weight_grad_kernel,
        grid=(steps,),
        in_specs=[
            pl.BlockSpec((N_DP, 2, N_Y, CAP, 2 * HD), lambda i: (0,) * 5),
            pl.BlockSpec((N_DP, 2, N_Y, CAP, 2 * HD), lambda i: (0,) * 5),
            pl.BlockSpec((N_Y, N_Q, PART // steps, ROWS), lambda i: (0, 0, i, 0)),
        ],
        out_specs=pl.BlockSpec((N_DP * N_Y // steps, 2 * SHARE, HD), lambda i: (i, 0, 0)),
        out_shape=jax.ShapeDtypeStruct((N_DP * N_Y, 2 * SHARE, HD), bf16),
        compiler_params=pltpu.CompilerParams(vmem_limit_bytes=VMEM_LIMIT),
        cost_estimate=pl.CostEstimate(flops=1400000000, bytes_accessed=7000000, transcendentals=0),
        name="weight_grad",
    )(kv_own, kv_other, xt)


def final_kernel(parts_ref, out_ref):
    for g in range(HEADS):
        summed = parts_ref[0, g].astype(f32)
        for b in range(1, N_DP):
            summed = summed + parts_ref[b, g].astype(f32)
        summed = summed * ((N_DP * GROUP) ** -0.5)
        out_ref[:, g * HD : (g + 1) * HD] = summed[:SHARE]
        out_ref[:, KVW + g * HD : KVW + (g + 1) * HD] = summed[SHARE:]


def final(parts):
    vmem = pl.BlockSpec(memory_space=pltpu.VMEM)
    return pl.pallas_call(
        final_kernel,
        in_specs=[vmem],
        out_specs=vmem,
        out_shape=jax.ShapeDtypeStruct((SHARE, 2 * KVW), f32),
        name="final_sum",
    )(parts)


def swap(array, axes):
    return lax.all_to_all(array, axes, split_axis=0, concat_axis=0, tiled=True)


def flip(array, m):
    return lax.ppermute(array, Q, [(i, i ^ m) for i in range(N_Q)])


def along_y(array, s):
    return lax.ppermute(array, "y", [(i, (i + s) % N_Y) for i in range(N_Y)])


def shards(loaded_x, dest_dp, dest_pos, queries, grad_out, kv_weight, kv_bias, lengths):
    half = np.power(np.float32(1000000.0), -np.arange(HD // 2, dtype=np.float32) * np.float32(2.0 / HD))
    freq = jnp.asarray(np.concatenate([half, half])[None, :].astype(np.float32))
    dest_dp = dest_dp.reshape(1, ROWS)

    barrier = lax.optimization_barrier

    pieces = cut(dest_dp, loaded_x, queries, grad_out)
    x, qd, xt = barrier((loaded_x, pieces[:N_Y], pieces[N_Y:]))
    xt = [xt[0]] + [flip(xt[m], m) for m in range(1, N_Q)]
    qd = [qd[0]] + [along_y(qd[s], s) for s in range(1, N_Y)]
    kv = project(lengths, dest_dp, dest_pos.reshape(1, ROWS), freq, kv_bias, x, kv_weight)
    kv, xt = barrier((kv, xt))
    xt = jnp.stack(xt)
    kv, xt, qd = barrier((kv, xt, qd))
    xt = lax.all_gather(xt, "y", axis=0)
    kv = swap(kv.reshape(-1, CAP, 3 * HD), ("zh", "x", "y", "zl")).reshape(N_DP, N_Y, 2, CAP, 3 * HD)
    kv_other = lax.ppermute(kv, "c", [(0, 1), (1, 0)])

    stay, back, ahead, *dkv, posn = attention(lengths, kv, kv_other, qd)
    angle = posn * freq
    cosine = jnp.cos(angle)
    sine = jnp.sin(angle) * jnp.where(jnp.arange(HD) < HD // 2, -1.0, 1.0).astype(f32)
    dkv = [dkv[0]] + [flip(dkv[m], m) for m in range(1, N_Q)]
    back, ahead = along_y(back, -1), along_y(ahead, 1)
    kv_grad = key_grad(dkv, cosine, sine)
    kv_grad = swap(kv_grad.reshape(-1, N_Y * CAP, 2 * HD), ("zh", "x", "zl")).reshape(N_DP, 2, N_Y, CAP, 2 * HD)
    last_dq, last_out = along_y(back[2:], -1), along_y(ahead[2:], 1)
    kv_grad, last_dq, last_out = barrier((kv_grad, last_dq, last_out))
    kv_grad_other = lax.ppermute(kv_grad, "c", [(0, 1), (1, 0)])
    dw = weight_grad(xt, kv_grad, kv_grad_other)
    dw, back, ahead = barrier((dw, back, ahead))
    dw = swap(dw, ("zh", "x", "y"))
    attention_out, query_grad = merge_heads(stay, back, ahead, last_dq, last_out)
    dw, attention_out, query_grad = barrier((dw, attention_out, query_grad))
    kv_weight_grad = final(dw.reshape(N_DP, HEADS, 2 * SHARE, HD))
    return attention_out, query_grad, kv_weight_grad


def solution(mesh):
    split = Mesh(mesh.devices.reshape(2, 4, N_Y, 2, 2), AXES)
    rows = P(AXES, None)
    return jax.shard_map(
        shards,
        mesh=split,
        in_specs=(rows, P(AXES), P(AXES), rows, rows, P(), P(), P()),
        out_specs=(rows, rows, rows),
        check_vma=False,
    )
```

```python
import functools

import jax
import jax.numpy as jnp
import numpy as np
from jax import lax
from jax.experimental import pallas as pl
from jax.experimental.pallas import tpu as pltpu
from jax.sharding import Mesh
from jax.sharding import PartitionSpec as P

D = 5120
HD = 128
HEADS = 4
REP = 5
NSEQ = 4
N_DP = 8
N_Y = 4
N_Q = 4
N_CTX = N_Y * N_Q
ROWS = 128
CAP = ROWS // N_DP
GROUP = N_CTX * ROWS
KVW = HEADS * HD
QH = REP * HD
SHARE = D // (N_DP * N_CTX)
PART = D // N_Q
COLS = 2560
TURN = 2560
CHUNK = 512
PAIR = 2 * ROWS
N_CHUNK = GROUP // CHUNK
MASKED = -1e30
SCALE = HD**-0.5
LOG2E = 1.4426950408889634
AXES = ("zh", "x", "y", "zl", "c")
DP = ("zh", "x")
Q = ("zl", "c")
bf16 = jnp.bfloat16
f32 = jnp.float32
VMEM_LIMIT = 56 * 1024 * 1024


def iota(shape, axis):
    return lax.broadcasted_iota(jnp.int32, shape, axis)


def dot(a, b):
    return jnp.dot(a, b, preferred_element_type=f32)


def starts_of(places, end_of):
    start = jnp.zeros_like(places)
    for j in range(NSEQ):
        end = end_of(j)
        start = jnp.maximum(start, jnp.where(end <= places, end, 0))
    return start


def coordinates():
    dp = lax.axis_index("zh") * 4 + lax.axis_index("x")
    return dp, lax.axis_index("y"), lax.axis_index("zl") * 2 + lax.axis_index("c")


def order_of(dp_row):
    one_hot = (dp_row == iota((N_DP, ROWS), 0)).astype(f32)
    before = (iota((ROWS, ROWS), 0) < iota((ROWS, ROWS), 1)).astype(bf16)
    earlier = dot(one_hot.astype(bf16), before)
    rank = jnp.sum(earlier * one_hot, axis=0, keepdims=True).astype(jnp.int32)
    slot = dp_row * CAP + rank
    return (iota((ROWS, ROWS), 0) == slot).astype(f32).astype(bf16)


def cut_kernel(dp_ref, x_ref, q_ref, d_ref, *refs):
    head_refs, piece_refs, order, pieces = refs[:N_Y], refs[N_Y : N_Y + N_Q], refs[-2], refs[-1]
    _, y, own = coordinates()

    @pl.when(pl.program_id(0) == 0)
    def _():
        order[...] = order_of(dp_ref[...])

    for s in range(N_Y):
        lanes = pl.ds(pl.multiple_of(lax.rem(y + s, N_Y) * QH, HD), QH)
        head_refs[s][0] = q_ref[:, lanes]
        head_refs[s][1] = d_ref[:, lanes]
    turned = dot(order[...], x_ref[...]).T
    for q in range(N_Q):
        rows = [turned[(j * N_Q + q) * SHARE : (j * N_Q + q + 1) * SHARE] for j in range(TURN // (N_Q * SHARE))]
        pieces[q] = jnp.concatenate(rows, axis=0).astype(bf16)
    for m in range(N_Q):
        piece_refs[m][...] = pieces[own ^ m]


def cut(dest_dp, x, queries, grad_out):
    steps = D // TURN
    rows = ROWS // steps
    return pl.pallas_call(
        cut_kernel,
        grid=(steps,),
        in_specs=[
            pl.BlockSpec((1, ROWS), lambda i: (0, 0)),
            pl.BlockSpec((ROWS, TURN), lambda i: (0, i)),
            pl.BlockSpec((rows, HEADS * QH), lambda i: (i, 0)),
            pl.BlockSpec((rows, HEADS * QH), lambda i: (i, 0)),
        ],
        out_specs=[pl.BlockSpec((2, rows, QH), lambda i: (0, i, 0))] * N_Y
        + [pl.BlockSpec((TURN // N_Q, ROWS), lambda i: (i, 0))] * N_Q,
        out_shape=[jax.ShapeDtypeStruct((2, ROWS, QH), bf16)] * N_Y
        + [jax.ShapeDtypeStruct((PART, ROWS), bf16)] * N_Q,
        scratch_shapes=[pltpu.VMEM((ROWS, ROWS), bf16), pltpu.VMEM((N_Q, TURN // N_Q, ROWS), bf16)],
        compiler_params=pltpu.CompilerParams(vmem_limit_bytes=VMEM_LIMIT),
        cost_estimate=pl.CostEstimate(flops=2000000000, bytes_accessed=5200000, transcendentals=0),
        name="cut",
    )(dest_dp, x, queries, grad_out)


def merge_kernel(stay_ref, back_ref, ahead_ref, dq_ref, out_ref, *refs):
    y = lax.axis_index("y")
    pieces = [
        (stay_ref.at[0], stay_ref.at[1]),
        (back_ref.at[0], back_ref.at[1]),
        (out_ref.at[0], dq_ref.at[0]),
        (ahead_ref.at[0], ahead_ref.at[1]),
    ]
    for s in range(N_Y):
        lanes = pl.ds(pl.multiple_of(lax.rem(y + s, N_Y) * QH, HD), QH)
        for k in range(2):
            refs[k][:, lanes] = pieces[s][k][...]


def merge_heads(*pieces):
    vmem = pl.BlockSpec(memory_space=pltpu.VMEM)
    return pl.pallas_call(
        merge_kernel,
        in_specs=[vmem] * len(pieces),
        out_specs=[vmem] * 2,
        out_shape=[jax.ShapeDtypeStruct((ROWS, HEADS * QH), bf16)] * 2,
        name="merge_heads",
    )(*pieces)


def project_kernel(lengths_ref, dp_ref, pos_ref, freq_ref, bias_ref, x_ref, w_ref, kv_ref, total):
    step = pl.program_id(0)

    @pl.when(step == 0)
    def _():
        total[...] = jnp.zeros_like(total)

    total[...] += dot(x_ref[...], w_ref[...])

    @pl.when(step == pl.num_programs(0) - 1)
    def _():
        _, y, q = coordinates()

        def column(row):
            diagonal = iota((ROWS, ROWS), 0) == iota((ROWS, ROWS), 1)
            picked = jnp.sum(jnp.where(diagonal, row.astype(f32), 0.0), axis=1, keepdims=True)
            return jnp.broadcast_to(picked, (ROWS, HD)).astype(jnp.int32)

        group = column(dp_ref[...])
        pos = column(pos_ref[...])
        places = pos + (y * N_Q + q) * ROWS
        ends = jnp.zeros((N_DP, 1), jnp.int32)
        columns = []
        for j in range(NSEQ):
            ends = ends + lengths_ref[:, j : j + 1]
            columns.append(ends)

        def end_of(j):
            end = jnp.zeros((ROWS, HD), jnp.int32)
            for b in range(N_DP):
                end = jnp.where(group == b, columns[j][b : b + 1], end)
            return end

        angle = (places - starts_of(places, end_of)).astype(f32) * freq_ref[...]
        cosine = jnp.cos(angle)
        sine = jnp.where(iota((ROWS, HD), 1) < HD // 2, -1.0, 1.0) * jnp.sin(angle)
        order = order_of(dp_ref[...])
        bias = bias_ref[...].reshape(1, 2 * KVW).astype(f32)
        pos = pos.astype(f32).astype(bf16)
        for g in range(HEADS):
            lanes = slice(g * HD, (g + 1) * HD)
            key = total[:, lanes] + bias[:, lanes]
            key = key * cosine + pltpu.roll(key, HD // 2, 1) * sine
            lanes = slice(KVW + g * HD, KVW + (g + 1) * HD)
            value = total[:, lanes] + bias[:, lanes]
            packed = jnp.concatenate([key.astype(bf16), value.astype(bf16), pos], axis=1)
            packed = dot(order, packed).astype(bf16)
            for b in range(N_DP):
                for z in range(2):
                    kv_ref[b, g, z] = packed[b * CAP : (b + 1) * CAP]


def project(lengths, dest_dp, dest_pos, freq, bias, x, w):
    whole = lambda *shape: pl.BlockSpec(shape, lambda i: (0,) * len(shape))
    return pl.pallas_call(
        project_kernel,
        grid=(D // COLS,),
        in_specs=[
            whole(N_DP, NSEQ),
            whole(1, ROWS),
            whole(1, ROWS),
            whole(1, HD),
            whole(2 * KVW),
            pl.BlockSpec((ROWS, COLS), lambda i: (0, i)),
            pl.BlockSpec((COLS, 2 * KVW), lambda i: (i, 0)),
        ],
        out_specs=whole(N_DP, HEADS, 2, CAP, 3 * HD),
        out_shape=jax.ShapeDtypeStruct((N_DP, HEADS, 2, CAP, 3 * HD), bf16),
        scratch_shapes=[pltpu.VMEM((ROWS, 2 * KVW), f32)],
        compiler_params=pltpu.CompilerParams(vmem_limit_bytes=VMEM_LIMIT),
        cost_estimate=pl.CostEstimate(flops=1600000000, bytes_accessed=16000000, transcendentals=0),
        name="project",
    )(lengths, dest_dp, dest_pos, freq, bias, x, w)


def attention_kernel(lengths_ref, kv_own_ref, kv_other_ref, *refs):
    qd_refs, refs = refs[:N_Y], refs[N_Y:]
    stay_ref, back_ref, ahead_ref = refs[:3]
    out_refs = [stay_ref.at[0], back_ref.at[0], ahead_ref.at[2], ahead_ref.at[0]]
    dq_refs = [stay_ref.at[1], back_ref.at[1], back_ref.at[2], ahead_ref.at[1]]
    dkv_refs = refs[3 : 3 + N_Q]
    posn_ref = refs[3 + N_Q]
    (keys, values, keys_t, values_t, places, probs, q_rows, d_rows, q_t, d_t,
                     out_t, dq_t, dk, dv) = refs[4 + N_Q :]
    own, y_own, q_own = coordinates()
    ends = []
    for j in range(NSEQ):
        counted = (iota((N_DP, NSEQ), 0) == own) & (iota((N_DP, NSEQ), 1) <= j)
        ends.append(jnp.sum(jnp.where(counted, lengths_ref[...], 0).astype(f32)).astype(jnp.int32))

    core = q_own % 2
    for kv_ref, c in ((kv_own_ref, core), (kv_other_ref, 1 - core)):
        for pair in range(GROUP // PAIR):
            block = kv_ref[:, pair // 2, pair % 2].reshape(ROWS, 3 * HD)
            first = pl.multiple_of(pair * PAIR + c * ROWS, ROWS)
            rows = pl.ds(first, ROWS)
            chunk = pair * PAIR // CHUNK
            lanes = pl.ds(pl.multiple_of(pair * PAIR % CHUNK + c * ROWS, ROWS), ROWS)
            key = block[:, :HD]
            value = block[:, HD : 2 * HD]
            keys[rows] = key
            values[rows] = value
            keys_t[chunk, :, lanes] = key.T
            values_t[chunk, :, lanes] = value.T
            places[rows] = block[:, 2 * HD :].astype(f32).astype(jnp.int32) + first
    dk[...] = jnp.zeros_like(dk)
    dv[...] = jnp.zeros_like(dv)

    for s in range(N_Y):
        qd_ref = qd_refs[s]
        own_places = places[pl.ds(pl.multiple_of((s * N_Q + q_own) * ROWS, ROWS), ROWS)]
        first = (lax.rem(y_own + N_Y - s, N_Y) * N_Q + q_own) * ROWS
        posn_ref[s] = (own_places - starts_of(own_places, lambda j: ends[j])).astype(f32)
        for h in range(REP):
            lanes = slice(h * HD, (h + 1) * HD)
            query = qd_ref[0, :, lanes]
            cotangent = qd_ref[1, :, lanes]
            q_rows[lanes] = query
            d_rows[lanes] = cotangent
            q_t[:, lanes] = query.T
            d_t[:, lanes] = cotangent.T
        row_places = first + iota((1, ROWS), 1)
        row_starts = starts_of(row_places, lambda j: ends[j])
        first_start = starts_of(first, lambda j: ends[j])
        low = first_start // CHUNK
        high = (first + ROWS - 1) // CHUNK + 1

        def rows_of(c):
            return pl.ds(pl.multiple_of(c * CHUNK, CHUNK), CHUNK)

        def score(c, top):
            at = rows_of(c)
            key_places = places[at]
            allowed = (key_places <= row_places) & (key_places >= row_starts)
            bias = jnp.where(allowed, 0.0, MASKED)
            s = dot(keys[at], q_t[...]) * (SCALE * LOG2E) + jnp.concatenate([bias] * REP, axis=1)
            probs[at] = s
            return jnp.maximum(top, jnp.max(s, axis=0, keepdims=True))

        top = lax.fori_loop(low, high, score, jnp.full((1, QH), MASKED, f32))
        out_t[...] = jnp.zeros_like(out_t)

        def add_out(c, summed):
            at = rows_of(c)
            p = jnp.exp2(probs[at] - top)
            probs[at] = p
            out_t[...] += dot(values_t[c], p.astype(bf16))
            return summed + jnp.sum(p, axis=0, keepdims=True)

        summed = lax.fori_loop(low, high, add_out, jnp.zeros((1, QH), f32))
        inverse = 1.0 / summed
        rounded = (out_t[...] * inverse).astype(bf16).astype(f32)
        delta = jnp.sum(d_t[...].astype(f32) * rounded, axis=0, keepdims=True)
        for h in range(REP):
            lanes = slice(h * HD, (h + 1) * HD)
            out_refs[s][:, lanes] = rounded[:, lanes].astype(bf16).T
        dq_t[...] = jnp.zeros_like(dq_t)

        def add_grad(c, carry):
            at = rows_of(c)
            w = probs[at] * inverse
            slope = (w * (dot(values[at], d_t[...]) - delta)).astype(bf16)
            dq_t[...] += dot(keys_t[c], slope)
            dk[at] += dot(slope, q_rows[...])
            dv[at] += dot(w.astype(bf16), d_rows[...])
            return carry

        lax.fori_loop(low, high, add_grad, 0)
        for h in range(REP):
            lanes = slice(h * HD, (h + 1) * HD)
            dq_refs[s][:, lanes] = (dq_t[:, lanes] * SCALE).astype(bf16).T

    for m in range(N_Q):
        for y in range(N_Y):
            rows = pl.ds(pl.multiple_of((y * N_Q + (q_own ^ m)) * ROWS, ROWS), ROWS)
            dkv_refs[m][y, :, :HD] = (dk[rows] * SCALE).astype(bf16)
            dkv_refs[m][y, :, HD:] = dv[rows].astype(bf16)


def attention(lengths, kv_own, kv_other, qd):
    vmem = pl.BlockSpec(memory_space=pltpu.VMEM)
    return pl.pallas_call(
        attention_kernel,
        in_specs=[vmem] * (3 + N_Y),
        out_specs=[vmem] * (4 + N_Q),
        out_shape=[jax.ShapeDtypeStruct((n, ROWS, QH), bf16) for n in (2, 3, 3)]
        + [jax.ShapeDtypeStruct((N_Y, ROWS, 2 * HD), bf16)] * N_Q
        + [jax.ShapeDtypeStruct((N_Y, ROWS, HD), f32)],
        scratch_shapes=[
            pltpu.VMEM((GROUP, HD), bf16),
            pltpu.VMEM((GROUP, HD), bf16),
            pltpu.VMEM((N_CHUNK, HD, CHUNK), bf16),
            pltpu.VMEM((N_CHUNK, HD, CHUNK), bf16),
            pltpu.VMEM((GROUP, HD), jnp.int32),
            pltpu.VMEM((GROUP, QH), f32),
            pltpu.VMEM((QH, HD), bf16),
            pltpu.VMEM((QH, HD), bf16),
            pltpu.VMEM((HD, QH), bf16),
            pltpu.VMEM((HD, QH), bf16),
            pltpu.VMEM((HD, QH), f32),
            pltpu.VMEM((HD, QH), f32),
            pltpu.VMEM((GROUP, HD), f32),
            pltpu.VMEM((GROUP, HD), f32),
        ],
        compiler_params=pltpu.CompilerParams(vmem_limit_bytes=VMEM_LIMIT),
        cost_estimate=pl.CostEstimate(flops=20000000000, bytes_accessed=8000000, transcendentals=3000000),
        name="attention",
    )(lengths, kv_own, kv_other, *qd)


def key_grad_kernel(cos_ref, sin_ref, *refs):
    out_ref = refs[N_Q]
    for y in range(N_Y):
        summed = refs[0][y].astype(f32)
        for q in range(1, N_Q):
            summed = summed + refs[q][y].astype(f32)
        key = summed[:, :HD]
        key = key * cos_ref[y] - pltpu.roll(key, HD // 2, 1) * sin_ref[y]
        both = jnp.concatenate([key, summed[:, HD:]], axis=1).astype(bf16)
        for b in range(N_DP):
            for z in range(2):
                out_ref[b, z, y] = both[b * CAP : (b + 1) * CAP]


def key_grad(parts, cosine, sine):
    vmem = pl.BlockSpec(memory_space=pltpu.VMEM)
    return pl.pallas_call(
        key_grad_kernel,
        in_specs=[vmem] * (2 + N_Q),
        out_specs=vmem,
        out_shape=jax.ShapeDtypeStruct((N_DP, 2, N_Y, CAP, 2 * HD), bf16),
        compiler_params=pltpu.CompilerParams(vmem_limit_bytes=VMEM_LIMIT),
        name="key_grad",
    )(cosine, sine, *parts)


def weight_grad_kernel(kv_own_ref, kv_other_ref, xt_ref, out_ref):
    zl = lax.axis_index("zl")
    total = None
    for y in range(N_Y):
        for z in range(2):
            kv = [ref[:, zl ^ z, y].reshape(ROWS, 2 * HD) for ref in (kv_own_ref, kv_other_ref)]
            left = jnp.concatenate([xt_ref[y, 2 * z], xt_ref[y, 2 * z + 1]], axis=1)
            term = dot(left, jnp.concatenate(kv, axis=0))
            total = term if total is None else total + term
    for j in range(out_ref.shape[0]):
        piece = total[j * SHARE : (j + 1) * SHARE]
        out_ref[j] = jnp.concatenate([piece[:, :HD], piece[:, HD:]], axis=0).astype(bf16)


def weight_grad(xt, kv_own, kv_other):
    steps = 1
    return pl.pallas_call(
        weight_grad_kernel,
        grid=(steps,),
        in_specs=[
            pl.BlockSpec((N_DP, 2, N_Y, CAP, 2 * HD), lambda i: (0,) * 5),
            pl.BlockSpec((N_DP, 2, N_Y, CAP, 2 * HD), lambda i: (0,) * 5),
            pl.BlockSpec((N_Y, N_Q, PART // steps, ROWS), lambda i: (0, 0, i, 0)),
        ],
        out_specs=pl.BlockSpec((N_DP * N_Y // steps, 2 * SHARE, HD), lambda i: (i, 0, 0)),
        out_shape=jax.ShapeDtypeStruct((N_DP * N_Y, 2 * SHARE, HD), bf16),
        compiler_params=pltpu.CompilerParams(vmem_limit_bytes=VMEM_LIMIT // 2),
        cost_estimate=pl.CostEstimate(flops=1400000000, bytes_accessed=7000000, transcendentals=0),
        name="weight_grad",
    )(kv_own, kv_other, xt)


def final_kernel(parts_ref, out_ref):
    for g in range(HEADS):
        summed = parts_ref[0, g].astype(f32)
        for b in range(1, N_DP):
            summed = summed + parts_ref[b, g].astype(f32)
        summed = summed * ((N_DP * GROUP) ** -0.5)
        out_ref[:, g * HD : (g + 1) * HD] = summed[:SHARE]
        out_ref[:, KVW + g * HD : KVW + (g + 1) * HD] = summed[SHARE:]


def final(parts):
    vmem = pl.BlockSpec(memory_space=pltpu.VMEM)
    return pl.pallas_call(
        final_kernel,
        in_specs=[vmem],
        out_specs=vmem,
        out_shape=jax.ShapeDtypeStruct((SHARE, 2 * KVW), f32),
        name="final_sum",
    )(parts)


def swap(array, axes):
    return lax.all_to_all(array, axes, split_axis=0, concat_axis=0, tiled=True)


def flip(array, m):
    return lax.ppermute(array, Q, [(i, i ^ m) for i in range(N_Q)])


def along_y(array, s):
    return lax.ppermute(array, "y", [(i, (i + s) % N_Y) for i in range(N_Y)])


def shards(loaded_x, dest_dp, dest_pos, queries, grad_out, kv_weight, kv_bias, lengths):
    half = np.power(np.float32(1000000.0), -np.arange(HD // 2, dtype=np.float32) * np.float32(2.0 / HD))
    freq = jnp.asarray(np.concatenate([half, half])[None, :].astype(np.float32))
    dest_dp = dest_dp.reshape(1, ROWS)

    barrier = lax.optimization_barrier

    pieces = cut(dest_dp, loaded_x, queries, grad_out)
    x, qd, xt = barrier((loaded_x, pieces[:N_Y], pieces[N_Y:]))
    xt = [xt[0]] + [flip(xt[m], m) for m in range(1, N_Q)]
    qd = [qd[0]] + [along_y(qd[s], s) for s in range(1, N_Y)]
    kv = project(lengths, dest_dp, dest_pos.reshape(1, ROWS), freq, kv_bias, x, kv_weight)
    kv, xt = barrier((kv, xt))
    xt = jnp.stack(xt)
    kv, xt, qd = barrier((kv, xt, qd))
    xt = lax.all_gather(xt, "y", axis=0)
    kv = swap(kv.reshape(-1, CAP, 3 * HD), ("zh", "x", "y", "zl")).reshape(N_DP, N_Y, 2, CAP, 3 * HD)
    kv_other = lax.ppermute(kv, "c", [(0, 1), (1, 0)])

    stay, back, ahead, *dkv, posn = attention(lengths, kv, kv_other, qd)
    angle = posn * freq
    cosine = jnp.cos(angle)
    sine = jnp.sin(angle) * jnp.where(jnp.arange(HD) < HD // 2, -1.0, 1.0).astype(f32)
    dkv = [dkv[0]] + [flip(dkv[m], m) for m in range(1, N_Q)]
    back, ahead = along_y(back, -1), along_y(ahead, 1)
    kv_grad = key_grad(dkv, cosine, sine)
    kv_grad = swap(kv_grad.reshape(-1, N_Y * CAP, 2 * HD), ("zh", "x", "zl")).reshape(N_DP, 2, N_Y, CAP, 2 * HD)
    last_dq, last_out = along_y(back[2:], -1), along_y(ahead[2:], 1)
    kv_grad, last_dq, last_out, xt = barrier((kv_grad, last_dq, last_out, xt))
    kv_grad_other = lax.ppermute(kv_grad, "c", [(0, 1), (1, 0)])
    dw = weight_grad(xt, kv_grad, kv_grad_other)
    dw, back, ahead = barrier((dw, back, ahead))
    dw = swap(dw, ("zh", "x", "y"))
    attention_out, query_grad = merge_heads(stay, back, ahead, last_dq, last_out)
    dw, attention_out, query_grad = barrier((dw, attention_out, query_grad))
    kv_weight_grad = final(dw.reshape(N_DP, HEADS, 2 * SHARE, HD))
    return attention_out, query_grad, kv_weight_grad


def solution(mesh):
    split = Mesh(mesh.devices.reshape(2, 4, N_Y, 2, 2), AXES)
    rows = P(AXES, None)
    return jax.shard_map(
        shards,
        mesh=split,
        in_specs=(rows, P(AXES), P(AXES), rows, rows, P(), P(), P()),
        out_specs=(rows, rows, rows),
        check_vma=False,
    )
```
